32 devices in a mesh: expert: 8 (over z, y), shard: 4 (over x, core).
Axes of the slice: x: 2, y: 2, z: 4, core: 2. Of those that a mesh axis runs over, the one named last changes fastest.
Arguments:
- inputs: bfloat16 [8192, 768], P('expert'), may hold values from -6 to 6
- cotangent: bfloat16 [8192, 768], P('expert'), may hold values from -6 to 6
- expert_id: int32 [8192], P('expert'), may hold values from 0 to 7, as said below
- slot_index: int32 [8192], P('expert'), may hold values from 0 to 256, as said below
- bucket_ids: int32 [1024, 1024], replicated, may hold values from 0 to 31, as said below
- attention_gain: float32 [768], replicated, may hold values from 0.5 to 1.5
- query_weight: bfloat16 [768, 768], P(None, 'shard'), may hold values from -0.21875 to 0.21875
- key_weight: bfloat16 [768, 768], P(None, 'shard'), may hold values from -0.21875 to 0.21875
- value_weight: bfloat16 [768, 768], P(None, 'shard'), may hold values from -0.21875 to 0.21875
- output_weight: bfloat16 [768, 768], P('shard'), may hold values from -3.5 to 3.5
- bias_table: float32 [32, 12], P(None, 'shard'), may hold values from -5 to 5
- expert_gain: float32 [768], replicated, may hold values from 0.5 to 1.5
- router_weight: bfloat16 [768, 8], replicated, may hold values from -0.109375 to 0.109375
- expert_in: bfloat16 [8, 768, 3072], P('expert', None, 'shard'), may hold values from -0.21875 to 0.21875
- expert_out: bfloat16 [8, 3072, 768], P('expert', 'shard'), may hold values from -12 to 12
Outputs:
- result: bfloat16 [8192, 768], P('expert')
- input_gradient: float32 [8192, 768], P('expert')
- attention_gain_gradient: float32 [768], replicated
- query_gradient: float32 [768, 768], P(None, 'shard')
- key_gradient: float32 [768, 768], P(None, 'shard')
- value_gradient: float32 [768, 768], P(None, 'shard')
- output_weight_gradient: float32 [768, 768], P('shard')
- bias_table_gradient: float32 [32, 12], P(None, 'shard')
- expert_gain_gradient: float32 [768], replicated
- router_gradient: float32 [768, 8], replicated
- expert_in_gradient: float32 [8, 768, 3072], P('expert', None, 'shard')
- expert_out_gradient: float32 [8, 3072, 768], P('expert', 'shard')
The draws below stay inside these ranges and needn't reach their ends.
Inputs may be any that keep to these rules, and one draw needn't show every extreme that they name: `expert_id`: in every sequence exactly 257 tokens go to one expert, the same one for all sequences; every other expert receives fewer tokens of a sequence than that. slot_index is the rank of the token, in some order, among the tokens of its sequence that go to the same expert; tokens whose slot_index is 192 or more are dropped. bucket_ids[a, c] depends only on c - a.
All inputs are finite; a program needn't handle non-finite values.
Results may differ from the reference program's by a relative error of at most 0.018.
Values may be sent and summed in bfloat16 or wider, within the bound.
No kernel may reach another device: no remote copies, remote signals or barrier semaphores. Data moves between devices by JAX's collectives and lax.ppermute only.
A program may use at most 192 MiB of HBM per device.

```python
import jax
import jax.numpy as jnp
from jax import lax

D = 768
HEADS = 12
DH = 64
FF = 3072
BUCKETS = 32
LEN = 1024
SEQS = 8
TOKENS = 8192
EXPERTS = 8
CAP = 192


def routing_pair(key):
    groups = TOKENS // LEN
    base_key = jax.random.fold_in(key, 7)
    key_hot, key_shift, key_order, key_warm, key_extra = jax.random.split(base_key, 5)
    hot_expert = jax.random.randint(key_hot, (), 0, EXPERTS).astype(jnp.int32)
    shifts = jax.random.randint(key_shift, (groups, 1), 0, EXPERTS - 1).astype(jnp.int32)
    orders = jax.vmap(lambda single: jax.random.permutation(single, LEN))(jax.random.split(key_order, groups))
    position = jnp.arange(LEN, dtype=jnp.int32)[None, :]
    hot_count = CAP + CAP // 3 + 1
    most_other = CAP + CAP // 3
    rest_all = LEN - hot_count
    base_share = (rest_all + EXPERTS - 2) // (EXPERTS - 1)
    upper = min(most_other - base_share, rest_all // 3)
    lower = (upper + 1) // 2
    extras = jax.random.randint(key_extra, (groups, 3), lower, upper + 1).astype(jnp.int32)
    extras = extras.at[:, 0].set(upper)
    warm_offsets = jax.vmap(lambda single: jax.random.permutation(single, EXPERTS - 1)[:3])(jax.random.split(key_warm, groups)).astype(jnp.int32)
    warm_ids = ((hot_expert + 1 + warm_offsets) % EXPERTS).astype(jnp.int32)
    bound_one = hot_count + extras[:, 0:1]
    bound_two = bound_one + extras[:, 1:2]
    bound_three = bound_two + extras[:, 2:3]
    cyclic = (hot_expert + 1 + (position - bound_three + shifts) % (EXPERTS - 1)) % EXPERTS
    ordered_ids = jnp.where(position < hot_count, hot_expert, jnp.where(position < bound_one, warm_ids[:, 0:1], jnp.where(position < bound_two, warm_ids[:, 1:2], jnp.where(position < bound_three, warm_ids[:, 2:3], cyclic))))
    ordered_ids = ordered_ids.astype(jnp.int32)
    indicator = (ordered_ids[:, :, None] == jnp.arange(EXPERTS, dtype=jnp.int32)[None, None, :]).astype(jnp.int32)
    ordered_ranks = jnp.sum((jnp.cumsum(indicator, axis=1) - 1) * indicator, axis=2).astype(jnp.int32)
    group_index = jnp.arange(groups, dtype=jnp.int32)[:, None]
    expert_ids = jnp.zeros((groups, LEN), jnp.int32).at[group_index, orders].set(ordered_ids)
    slot_ids = jnp.zeros((groups, LEN), jnp.int32).at[group_index, orders].set(ordered_ranks)
    return (expert_ids.reshape(TOKENS), slot_ids.reshape(TOKENS))


def draw_expert_id(key, part):
    return routing_pair(key)[0]


def draw_slot_index(key, part):
    return routing_pair(key)[1]


def draw_bucket_ids(key, part):
    offsets = jax.random.randint(jax.random.fold_in(key, 11), (2 * LEN - 1,), 0, BUCKETS).astype(jnp.int32)
    places = jnp.arange(LEN, dtype=jnp.int32)
    return offsets[places[None, :] - places[:, None] + LEN - 1]


def level_of(key, extent, pieces, least, largest):
    level = 1.0
    for axis_at, parts in pieces:
        steps = jax.random.uniform(jax.random.fold_in(jax.random.fold_in(key, 6), axis_at), (parts,), jnp.float32, least / len(pieces), largest / len(pieces))
        level = level * jnp.repeat(jnp.exp(steps), extent[axis_at] // parts).reshape((-1,) + (1,) * (len(extent) - 1 - axis_at))
    return level


def normal_values(rng, extent, scale, most, cuts=(), held_as=jnp.bfloat16):
    array = scale * jax.random.normal(rng, extent, jnp.float32)
    if cuts:
        array = array * level_of(rng, extent, cuts, -0.22, 0.18)
    return jnp.clip(array, -most, most).astype(held_as)


def setup_inputs(seed: int = 0) -> dict:
    key_of = jax.random.split(jax.random.key(seed), 16)
    return {
        "inputs": normal_values(key_of[0], (TOKENS, D), 1.0, 6.0, ((0, 8),)),
        "cotangent": normal_values(key_of[1], (TOKENS, D), 1.0, 6.0, ((0, 8),)),
        "expert_id": draw_expert_id(jax.random.fold_in(key_of[15], 71), 0),
        "slot_index": draw_slot_index(jax.random.fold_in(key_of[15], 71), 0),
        "bucket_ids": draw_bucket_ids(jax.random.fold_in(key_of[15], 71), 0),
        "attention_gain": jnp.clip(1.0 + 0.1 * jax.random.normal(key_of[5], (D,), jnp.float32), 0.5, 1.5),
        "query_weight": normal_values(key_of[6], (D, D), D ** -0.5, 0.21875, ((1, 4),)),
        "key_weight": normal_values(key_of[7], (D, D), D ** -0.5, 0.21875, ((1, 4),)),
        "value_weight": normal_values(key_of[8], (D, D), D ** -0.5, 0.21875, ((1, 4),)),
        "output_weight": normal_values(key_of[9], (D, D), (max(D // 256, 1)) ** -0.5, 3.5, ((0, 4),)),
        "bias_table": normal_values(key_of[10], (BUCKETS, HEADS), 1.0, 5.0, ((1, 4),), jnp.float32),
        "expert_gain": jnp.clip(1.0 + 0.1 * jax.random.normal(key_of[11], (D,), jnp.float32), 0.5, 1.5),
        "router_weight": normal_values(key_of[12], (D, EXPERTS), (4 * D) ** -0.5, 0.109375),
        "expert_in": normal_values(key_of[13], (EXPERTS, D, FF), D ** -0.5, 0.21875, ((0, 8), (2, 4))),
        "expert_out": normal_values(key_of[14], (EXPERTS, FF, D), 2.0, 12.0, ((0, 8), (1, 4))),
    }


highest = lax.Precision.HIGHEST

@jax.custom_vjp
def low(v):
    return lax.optimization_barrier(v.astype(jnp.bfloat16)).astype(jnp.float32)

@jax.custom_vjp
def low_back(v):
    return v

def low_keep(v):
    return (low(v), None)

def low_pass(kept, grad):
    return (grad,)

def back_keep(v):
    return (v, None)

def back_low(kept, grad):
    return (low(grad),)
low.defvjp(low_keep, low_pass)
low_back.defvjp(back_keep, back_low)

def rms_norm(values, gain_values):
    return values * lax.rsqrt(lax.optimization_barrier(jnp.mean(values * values, axis=-1, keepdims=True)) + 1e-06) * gain_values

def matmul(left_side, right_side):
    return jnp.dot(left_side, right_side, precision=highest)

def attend(queries, keys_all, values_all, bias_blocks):
    block_rows = min(512, LEN)
    block_count = LEN // block_rows

    def one_sequence(packed):
        query_seq, key_seq, value_seq = packed
        query_blocks = query_seq.reshape(block_count, block_rows, HEADS, DH)

        def one_block(inner):
            query_block, bias_block = inner
            scores = jnp.einsum('rhd,khd->hrk', query_block, key_seq, precision=highest) * 0.125 + bias_block
            scores = low_back(scores)
            weights = low(jax.nn.softmax(scores, axis=-1))
            return jnp.einsum('hrk,khd->rhd', weights, value_seq, precision=highest)
        return lax.map(jax.checkpoint(one_block), (query_blocks, bias_blocks)).reshape(LEN, HEADS, DH)
    return lax.map(jax.checkpoint(one_sequence), (queries, keys_all, values_all))

def expert_block(packed):
    rows_in, weight_in, weight_out = packed
    before = low_back(matmul(rows_in, weight_in))
    hidden = low(jax.nn.gelu(before, approximate=True))
    return low_back(low(matmul(hidden, weight_out)))

def forward(inputs, attention_gain, query_weight, key_weight, value_weight, output_weight, bias_table, expert_gain, router_weight, expert_in, expert_out, expert_id, slot_index, bucket_ids):
    block_rows = min(512, LEN)
    block_count = LEN // block_rows
    normed = low(rms_norm(inputs, attention_gain))
    queries = low_back(low(matmul(normed, query_weight)))
    keys_all = low_back(low(matmul(normed, key_weight)))
    values_all = low_back(low(matmul(normed, value_weight)))
    split_shape = (SEQS, LEN, HEADS, DH)
    bias_full = jnp.transpose(bias_table[bucket_ids], (2, 0, 1))
    bias_blocks = jnp.transpose(bias_full.reshape(HEADS, block_count, block_rows, LEN), (1, 0, 2, 3))
    mixed = attend(queries.reshape(split_shape), keys_all.reshape(split_shape), values_all.reshape(split_shape), bias_blocks)
    mixed = low_back(low(mixed.reshape(TOKENS, HEADS * DH)))
    attention = low_back(matmul(mixed, output_weight))
    middle = inputs + attention
    routed = low(rms_norm(middle, expert_gain))
    logits = low_back(matmul(routed, router_weight))
    probability = jax.nn.softmax(logits, axis=-1)
    chosen_mask = (expert_id[:, None] == jnp.arange(EXPERTS, dtype=jnp.int32)[None, :]).astype(jnp.float32)
    gate_value = lax.optimization_barrier(jnp.sum(probability * chosen_mask, axis=-1))
    sequence_of = jnp.arange(TOKENS, dtype=jnp.int32) // LEN
    target = jnp.where(slot_index < CAP, (expert_id * SEQS + sequence_of) * CAP + slot_index, EXPERTS * SEQS * CAP).astype(jnp.int32)
    buffer = jnp.zeros((EXPERTS * SEQS * CAP + 1, D), jnp.float32).at[target].add(routed)
    buffer = low_back(buffer[:-1].reshape(EXPERTS, SEQS * CAP, D))
    outcome = lax.map(jax.checkpoint(expert_block), (buffer, expert_in, expert_out))
    padded = jnp.concatenate([outcome.reshape(EXPERTS * SEQS * CAP, D), jnp.zeros((1, D), jnp.float32)], axis=0)
    return middle + gate_value[:, None] * padded[target]

def reference(inputs, cotangent, expert_id, slot_index, bucket_ids, attention_gain, query_weight, key_weight, value_weight, output_weight, bias_table, expert_gain, router_weight, expert_in, expert_out):

    def closed(*weights_all):
        return forward(*weights_all, expert_id, slot_index, bucket_ids)
    floats = (inputs, attention_gain, query_weight, key_weight, value_weight, output_weight, bias_table, expert_gain, router_weight, expert_in, expert_out)
    floats = tuple((item.astype(jnp.float32) for item in floats))
    result, pullback = jax.vjp(closed, *floats)
    grads_all = pullback(cotangent.astype(jnp.float32))
    return (result.astype(jnp.bfloat16), grads_all[0], grads_all[1], grads_all[2], grads_all[3], grads_all[4], grads_all[5], grads_all[6], grads_all[7], grads_all[8], grads_all[9], grads_all[10])
```

```python
import functools
import jax
import jax.numpy as jnp
from jax import lax
from jax.experimental import pallas as pl
from jax.experimental.pallas import tpu as pltpu
from jax.sharding import PartitionSpec as P

VMEM_LIMIT = 56 * 1024 * 1024


def dot(a, b, ca=1, cb=0):
    return lax.dot_general(a, b, (((ca,), (cb,)), ((), ())), preferred_element_type=jnp.float32)


def bias_strip(values_row, rows):
    total = values_row.shape[-1]
    wide = jnp.broadcast_to(values_row.reshape(1, total), (rows, total))
    return pltpu.roll(wide, total - rows + 1, 1, stride=1, stride_axis=0)


def attention_forward_kernel(heads, head_size, rows, in_ref, gain_ref, wq_ref, wk_ref, wv_ref, bias_ref, mixed_ref, qkv_ref, normed_ref, strip_ref):
    length = in_ref.shape[0]
    blocks = length // rows
    hd = heads * head_size
    source = in_ref[...].astype(jnp.float32)
    inverse = lax.rsqrt(jnp.mean(source * source, axis=1, keepdims=True) + 1e-06)
    normed_ref[...] = (source * inverse * gain_ref[...]).astype(jnp.bfloat16)
    for at, ref in enumerate((wq_ref, wk_ref, wv_ref)):
        qkv_ref[at * hd : (at + 1) * hd, :] = dot(ref[...], normed_ref[...], 0, 1).astype(jnp.bfloat16)
    for h in range(heads):
        strip_ref[...] = bias_strip(bias_ref[h : h + 1, :], rows)
        q = (qkv_ref[h * head_size : (h + 1) * head_size, :].astype(jnp.float32) * 0.125).T.astype(jnp.bfloat16)
        kt = qkv_ref[hd + h * head_size : hd + (h + 1) * head_size, :]
        vt = qkv_ref[2 * hd + h * head_size : 2 * hd + (h + 1) * head_size, :]
        for i in range(blocks):
            s = dot(q[i * rows : (i + 1) * rows], kt)
            at = (blocks - 1 - i) * rows
            s = s + strip_ref[:, at : at + length]
            peak = jnp.max(s, axis=1, keepdims=True)
            p = jnp.exp(s - peak)
            total = jnp.sum(p, axis=1, keepdims=True)
            o = dot(p.astype(jnp.bfloat16), vt, 1, 1) / total
            mixed_ref[h * head_size : (h + 1) * head_size, i * rows : (i + 1) * rows] = o.T.astype(jnp.bfloat16)


def in_vmem(count):
    return [pl.BlockSpec(memory_space=pltpu.VMEM)] * count


def attention_forward(inputs, gain, wq, wk, wv, bias_values, heads, head_size, rows=256):
    length = inputs.shape[0]
    hd = heads * head_size
    return pl.pallas_call(
        functools.partial(attention_forward_kernel, heads, head_size, rows),
        out_shape=(
            jax.ShapeDtypeStruct((hd, length), jnp.bfloat16),
            jax.ShapeDtypeStruct((3 * hd, length), jnp.bfloat16),
            jax.ShapeDtypeStruct(inputs.shape, jnp.bfloat16),
        ),
        in_specs=in_vmem(6),
        out_specs=tuple(in_vmem(3)),
        scratch_shapes=[pltpu.VMEM((rows, bias_values.shape[1]), jnp.float32)],
        compiler_params=pltpu.CompilerParams(vmem_limit_bytes=VMEM_LIMIT),
        cost_estimate=pl.CostEstimate(flops=10**10, bytes_accessed=10**7, transcendentals=heads * length * length),
        name="attention_forward",
    )(inputs, gain, wq, wk, wv, bias_values)


def call(body, out_shape, args, name, flops, scratch=(), transcendentals=0):
    return pl.pallas_call(
        body,
        out_shape=out_shape,
        in_specs=in_vmem(len(args)),
        out_specs=jax.tree.map(lambda _: in_vmem(1)[0], out_shape),
        scratch_shapes=list(scratch),
        compiler_params=pltpu.CompilerParams(vmem_limit_bytes=VMEM_LIMIT),
        cost_estimate=pl.CostEstimate(flops=flops, bytes_accessed=10**7, transcendentals=transcendentals),
        name=name,
    )(*args)


def shape(dims, dtype=jnp.bfloat16):
    return jax.ShapeDtypeStruct(dims, dtype)


def join(refs, target):
    at = 0
    for ref in refs:
        target[at : at + ref.shape[0], :] = ref[...]
        at += ref.shape[0]


def route_tokens(mixed_pieces, ow_pieces, source, pack, gain, router, sizes):
    shards = len(mixed_pieces)
    tokens, width = source.shape

    def body(*refs):
        mixed_refs, ow_refs = refs[:shards], refs[shards : 2 * shards]
        source_ref, pack_ref, gain_ref, router_ref = refs[2 * shards : 2 * shards + 4]
        middle_ref, routed_ref, probability_ref = refs[2 * shards + 4 : 2 * shards + 7]
        middle = source_ref[...]
        for m, o in zip(mixed_refs, ow_refs):
            middle = middle + dot(m[...], o[...])
        middle_ref[...] = middle
        spread = lax.rsqrt(jnp.mean(middle * middle, axis=1, keepdims=True) + 1e-06)
        routed = (middle * spread * gain_ref[...]).astype(jnp.bfloat16)
        routed_ref[...] = routed
        packed = dot(pack_ref[...], routed).astype(jnp.bfloat16)
        at = 0
        for ref in refs[2 * shards + 7 :]:
            ref[...] = packed[at : at + ref.shape[0], :]
            at += ref.shape[0]
        logits = dot(routed, router_ref[...])
        powered = jnp.exp(logits - jnp.max(logits, axis=1, keepdims=True))
        probability_ref[...] = powered / jnp.sum(powered, axis=1, keepdims=True)

    out = (shape((tokens, width), jnp.float32), shape((tokens, width)), shape((tokens, router.shape[1]), jnp.float32))
    out = out + tuple(shape((n, width)) for n in sizes)
    args = (*mixed_pieces, *ow_pieces, source, pack, gain, router)
    return call(body, out, args, "route_tokens", 10**9)


def expert_forward(pieces, grads, router, mine, w_in, w_out):
    count, width = grads.shape
    n, k_all = len(pieces), len(w_in)

    def body(*refs):
        piece_refs = refs[:n]
        grads_ref, router_ref, mine_ref = refs[n : n + 3]
        in_refs, out_refs = refs[n + 3 : n + 3 + k_all], refs[n + 3 + k_all : n + 3 + 2 * k_all]
        slope_ref, both_ref = refs[n + 3 + 2 * k_all : n + 5 + 2 * k_all]
        join(piece_refs, both_ref)
        rows = both_ref[:count, :]
        logits = dot(rows, router_ref[...])
        powered = jnp.exp(logits - jnp.max(logits, axis=1, keepdims=True))
        gate = jnp.sum(powered * mine_ref[...], axis=1, keepdims=True) / jnp.sum(powered, axis=1, keepdims=True)
        both_ref[count:, :] = (gate * grads_ref[...].astype(jnp.float32)).astype(jnp.bfloat16)
        total = jnp.zeros((count, width), jnp.float32)
        for k in range(k_all):
            value, slope = gelu_pair(dot(rows, in_refs[k][...]))
            slope_ref[:, k * width : (k + 1) * width] = slope.astype(jnp.bfloat16)
            total = total + dot(value.astype(jnp.bfloat16), out_refs[k][...])
        total = total.astype(jnp.bfloat16)
        at = 0
        for ref in refs[n + 5 + 2 * k_all :]:
            ref[...] = total[at : at + ref.shape[0], :]
            at += ref.shape[0]

    out = (shape((count, k_all * width)), shape((2 * count, width))) + tuple(shape(p.shape) for p in pieces)
    args = (*pieces, grads, router, mine, *w_in, *w_out)
    return call(body, out, args, "expert_forward", 4 * 10**9, transcendentals=count * 4 * width)


def expert_backward(both, slope, w_in, w_out, sizes):
    count, width = slope.shape[0], both.shape[1]
    k_all = len(w_in)

    def body(both_ref, slope_ref, *refs):
        in_refs, out_refs = refs[:k_all], refs[k_all : 2 * k_all]
        grads = both_ref[count:, :]
        total = jnp.zeros((count, width), jnp.float32)
        for k in range(k_all):
            part_slope = slope_ref[:, k * width : (k + 1) * width].astype(jnp.float32)
            before_grad = (dot(grads, out_refs[k][...], 1, 1) * part_slope).astype(jnp.bfloat16)
            total = total + dot(before_grad, in_refs[k][...], 1, 1)
        total = total.astype(jnp.bfloat16)
        at = 0
        for ref in refs[2 * k_all :]:
            ref[...] = total[at : at + ref.shape[0], :]
            at += ref.shape[0]

    out = tuple(shape((n, width)) for n in sizes)
    return call(body, out, (both, slope, *w_in, *w_out), "expert_backward", 4 * 10**9)


def token_grads(back_rows, back_grads, pack_t, middle, routed, probability, chosen, grad, gain, router, ow_pieces):
    tokens, width = middle.shape
    n, shards = len(back_rows), len(ow_pieces)
    hd = ow_pieces[0].shape[0]

    def body(*refs):
        row_refs, grad_refs = refs[:n], refs[n : 2 * n]
        pack_ref, middle_ref, routed_ref, probability_ref, chosen_ref, g_ref, gain_ref, router_ref = refs[2 * n : 2 * n + 8]
        ow_refs = refs[2 * n + 8 : 2 * n + 8 + shards]
        token_ref, router_part_ref, gain_part_ref = refs[2 * n + 8 + shards : 2 * n + 11 + shards]
        mixed_refs = refs[2 * n + 11 + shards : 2 * n + 11 + 2 * shards]
        buffer = refs[-1]
        g = g_ref[...].astype(jnp.float32)
        middle = middle_ref[...]
        chosen = chosen_ref[...]
        probability = probability_ref[...]
        gate = jnp.sum(probability * chosen, axis=1, keepdims=True)
        join(row_refs, buffer)
        rows = dot(pack_ref[...], buffer[...])
        token_ref[:, :width] = (middle + gate * rows).astype(jnp.bfloat16)
        gate_grad = jnp.sum(g * rows, axis=1, keepdims=True)
        logit_grad = (gate_grad * gate * (chosen - probability)).astype(jnp.bfloat16)
        router_part_ref[...] = dot(routed_ref[...], logit_grad, 0, 0)
        join(grad_refs, buffer)
        routed_grad = dot(logit_grad, router_ref[...], 1, 1) + dot(pack_ref[...], buffer[...])
        spread = lax.rsqrt(jnp.mean(middle * middle, axis=1, keepdims=True) + 1e-06)
        gain_part_ref[...] = jnp.sum(routed_grad * middle * spread, axis=0, keepdims=True)
        u = routed_grad * gain_ref[...]
        mean = jnp.mean(u * middle, axis=1, keepdims=True)
        middle_grad = (g + spread * u - middle * (spread * spread * spread * mean)).astype(jnp.bfloat16)
        token_ref[:, width:] = middle_grad
        for m, o in zip(mixed_refs, ow_refs):
            m[...] = dot(middle_grad, o[...], 1, 1).astype(jnp.bfloat16)

    out = (
        shape((tokens, 2 * width)),
        shape((width, router.shape[1]), jnp.float32),
        shape((1, width), jnp.float32),
    ) + (shape((tokens, hd)),) * shards
    args = (*back_rows, *back_grads, pack_t, middle, routed, probability, chosen, grad, gain, router, *ow_pieces)
    scratch = [pltpu.VMEM((pack_t.shape[1], width), jnp.bfloat16)]
    return call(body, out, args, "token_grads", 2 * 10**9, scratch)


def first_parts(normed, head_grads, weights, high):
    length, width = normed.shape
    rows = head_grads[0].shape[0]
    columns = rows * len(head_grads)
    half = width // 2

    def body(high_ref, normed_ref, weights_ref, *refs):
        keep_ref, sent_ref, gain_ref, part = refs[len(head_grads) :]
        for i, ref in enumerate(refs[: len(head_grads)]):
            part[:, i * rows : (i + 1) * rows] = dot(normed_ref[...], ref[...], 0, 1)
        gain_ref[...] = jnp.sum(weights_ref[...].astype(jnp.float32) * part[...], axis=1, keepdims=True)
        bit = high_ref[0]
        keep_ref[...] = part[pl.ds(pl.multiple_of(bit * half, half), half), :]
        sent_ref[...] = part[pl.ds(pl.multiple_of((1 - bit) * half, half), half), :].astype(jnp.bfloat16)

    out = (shape((half, columns), jnp.float32), shape((half, columns)), shape((width, 1), jnp.float32))
    return with_bit(body, out, (normed, weights, *head_grads), high, "first_parts", [pltpu.VMEM((width, columns), jnp.float32)])


def with_bit(body, out, args, high, name, scratch=()):
    return pl.pallas_call(
        body,
        out_shape=out,
        in_specs=[pl.BlockSpec(memory_space=pltpu.SMEM)] + in_vmem(len(args)),
        out_specs=jax.tree.map(lambda _: in_vmem(1)[0], out),
        scratch_shapes=list(scratch),
        compiler_params=pltpu.CompilerParams(vmem_limit_bytes=VMEM_LIMIT),
        cost_estimate=pl.CostEstimate(flops=2 * 10**9, bytes_accessed=10**7, transcendentals=0),
        name=name,
    )(high, *args)


def last_parts(normed, head_grad, weights, gain_before, gain, middle_grad, mixed_t, small, high):
    length, width = normed.shape
    rows, hd = head_grad.shape[0], mixed_t.shape[0]
    columns = rows + hd + small.shape[1]
    half = width // 2

    def body(high_ref, normed_ref, head_ref, weights_ref, before_ref, gain_ref, middle_ref, mixed_ref, small_ref, keep_ref, sent_ref, part):
        head_part = dot(normed_ref[...], head_ref[...], 0, 1)
        part[:, :rows] = head_part
        part[:, rows : rows + hd] = dot(middle_ref[...], mixed_ref[...], 0, 1)
        total = before_ref[...] + jnp.sum(weights_ref[...].astype(jnp.float32) * head_part, axis=1, keepdims=True)
        lane = lax.broadcasted_iota(jnp.int32, small_ref.shape, 1)
        part[:, rows + hd :] = jnp.where(lane == 0, total / gain_ref[...], small_ref[...])
        bit = high_ref[0]
        keep_ref[...] = part[pl.ds(pl.multiple_of(bit * half, half), half), :]
        sent_ref[...] = part[pl.ds(pl.multiple_of((1 - bit) * half, half), half), :].astype(jnp.bfloat16)

    out = (shape((half, columns), jnp.float32), shape((half, columns)))
    args = (normed, head_grad, weights, gain_before, gain, middle_grad, mixed_t, small)
    return with_bit(body, out, args, high, "last_parts", [pltpu.VMEM((width, columns), jnp.float32)])


def place_sums(first, last, high_first, high_last, heads, head_size):
    half, wide = first[0].shape
    width = 2 * half
    hd = heads * head_size
    extra = last[0].shape[1] - 3 * head_size - hd

    def body(first_bit, last_bit, a0, a1, b0, b1, q_ref, k_ref, v_ref, o_ref, small_ref):
        for i, (own, other) in enumerate(((a0, a1), (b0, b1))):
            bit = (first_bit, last_bit)[i][0]
            for ref, place in ((own, bit), (other, 1 - bit)):
                at = pl.ds(pl.multiple_of(place * half, half), half)
                value = ref[...].astype(jnp.float32)
                count = wide // (3 * head_size) if i == 0 else 1
                for j in range(count):
                    h = j if i == 0 else heads - 1
                    for c, out_ref in enumerate((q_ref, k_ref, v_ref)):
                        start = (3 * j + c) * head_size
                        out_ref[at, h * head_size : (h + 1) * head_size] = value[:, start : start + head_size]
                if i == 1:
                    o_ref[:, at] = value[:, 3 * head_size : 3 * head_size + hd].T
                    small_ref[at, :] = value[:, 3 * head_size + hd :]

    out = (shape((width, hd), jnp.float32),) * 3 + (shape((hd, width), jnp.float32), shape((width, extra), jnp.float32))
    return pl.pallas_call(
        body,
        out_shape=out,
        in_specs=[pl.BlockSpec(memory_space=pltpu.SMEM)] * 2 + in_vmem(4),
        out_specs=tuple(in_vmem(5)),
        compiler_params=pltpu.CompilerParams(vmem_limit_bytes=VMEM_LIMIT),
        cost_estimate=pl.CostEstimate(flops=10**6, bytes_accessed=10**7, transcendentals=0),
        name="place_sums",
    )(high_first, high_last, *first, *last)


def expert_weights_kernel(shards, count, all_ref, wi_ref, wo_ref, in_ref, out_ref):
    for s in range(shards):
        rows = all_ref[2 * s * count : (2 * s + 1) * count, :]
        grads = all_ref[(2 * s + 1) * count : (2 * s + 2) * count, :]
        value, slope = gelu_pair(dot(rows, wi_ref[...]))
        before_grad = (dot(grads, wo_ref[...], 1, 1) * slope).astype(jnp.bfloat16)
        part_in = dot(rows, before_grad, 0, 0)
        part_out = dot(value.astype(jnp.bfloat16), grads, 0, 0)
        if s == 0:
            in_ref[...] = part_in
            out_ref[...] = part_out
        else:
            in_ref[...] += part_in
            out_ref[...] += part_out


def expert_weights(everything, w_in, w_out, shards):
    count = everything.shape[0] // (2 * shards)
    return pl.pallas_call(
        functools.partial(expert_weights_kernel, shards, count),
        out_shape=(
            jax.ShapeDtypeStruct(w_in.shape, jnp.float32),
            jax.ShapeDtypeStruct(w_out.shape, jnp.float32),
        ),
        in_specs=in_vmem(3),
        out_specs=tuple(in_vmem(2)),
        compiler_params=pltpu.CompilerParams(vmem_limit_bytes=VMEM_LIMIT),
        cost_estimate=pl.CostEstimate(flops=10**10, bytes_accessed=10**7, transcendentals=10**6),
        name="expert_weights",
    )(everything, w_in, w_out)


def attention_backward_kernel(h, heads, head_size, rows, qkv_ref, bias_ref, grad_ref, out_ref, diag_ref, strip_ref, total_ref):
    length = qkv_ref.shape[1]
    blocks = length // rows
    hd = heads * head_size
    width = bias_ref.shape[1]
    strip_ref[...] = bias_strip(bias_ref[h : h + 1, :], rows)
    total_ref[...] = jnp.zeros_like(total_ref)
    qt32 = qkv_ref[h * head_size : (h + 1) * head_size, :].astype(jnp.float32) * 0.125
    qt = qt32.astype(jnp.bfloat16)
    q = qt32.T.astype(jnp.bfloat16)
    kt = qkv_ref[hd + h * head_size : hd + (h + 1) * head_size, :]
    k = kt.astype(jnp.float32).T.astype(jnp.bfloat16)
    vt = qkv_ref[2 * hd + h * head_size : 2 * hd + (h + 1) * head_size, :]
    gt = grad_ref[h * head_size : (h + 1) * head_size, :]
    g = gt.astype(jnp.float32).T.astype(jnp.bfloat16)
    dk = jnp.zeros((head_size, length), jnp.float32)
    dv = jnp.zeros((head_size, length), jnp.float32)
    for i in range(blocks):
        at = (blocks - 1 - i) * rows
        part = slice(i * rows, (i + 1) * rows)
        s = dot(q[part], kt) + strip_ref[:, at : at + length]
        peak = jnp.max(s, axis=1, keepdims=True)
        p = jnp.exp(s - peak)
        p = p * (1.0 / jnp.sum(p, axis=1, keepdims=True))
        dp = dot(g[part], vt)
        delta = jnp.sum(p * dp, axis=1, keepdims=True)
        ds = p * (dp - delta)
        total_ref[:, at : at + length] += ds
        dsb = ds.astype(jnp.bfloat16)
        dv = dv + dot(gt[:, part], p.astype(jnp.bfloat16))
        dk = dk + dot(qt[:, part], dsb)
        dq = dot(dsb, k) * 0.125
        out_ref[0:head_size, part] = dq.T.astype(jnp.bfloat16)
    out_ref[head_size : 2 * head_size, :] = dk.astype(jnp.bfloat16)
    out_ref[2 * head_size : 3 * head_size, :] = dv.astype(jnp.bfloat16)
    folded = total_ref[...]
    half = rows // 2
    while half:
        folded = folded[:half] + pltpu.roll(folded[half:], width - half, 1)
        half //= 2
    diag_ref[...] = pltpu.roll(folded, rows - 1, 1)


def attention_backward(qkv_t, bias_values, grad_t, h, heads, head_size, rows=256):
    length = qkv_t.shape[1]
    width = bias_values.shape[1]
    return pl.pallas_call(
        functools.partial(attention_backward_kernel, h, heads, head_size, rows),
        out_shape=(jax.ShapeDtypeStruct((3 * head_size, length), jnp.bfloat16), jax.ShapeDtypeStruct((1, width), jnp.float32)),
        in_specs=[pl.BlockSpec(memory_space=pltpu.VMEM)] * 3,
        out_specs=(pl.BlockSpec(memory_space=pltpu.VMEM),) * 2,
        scratch_shapes=[pltpu.VMEM((rows, width), jnp.float32)] * 2,
        compiler_params=pltpu.CompilerParams(vmem_limit_bytes=VMEM_LIMIT),
        cost_estimate=pl.CostEstimate(flops=10 * length * length * head_size * 8, bytes_accessed=4 * qkv_t.size, transcendentals=length * length),
        name="attention_backward",
    )(qkv_t, bias_values, grad_t)


def gelu_pair(v):
    inner = 0.7978845608028654 * (v + 0.044715 * v * v * v)
    t = jnp.tanh(inner)
    slope = 0.7978845608028654 * (1.0 + 3.0 * 0.044715 * v * v)
    return 0.5 * v * (1.0 + t), 0.5 * (1.0 + t) + 0.5 * v * (1.0 - t * t) * slope


def swap(x, axis, k):
    return lax.ppermute(x, axis, [(i, i ^ k) for i in range(lax.axis_size(axis))])


def gather_relative(x, axis="shard"):
    pieces = {0: x}
    bit = lax.axis_size(axis) // 2
    while bit:
        for k in sorted(pieces):
            pieces[k ^ bit] = swap(pieces[k], axis, bit)
        bit //= 2
    return [pieces[k] for k in range(len(pieces))]


def exchange_relative(pieces, axis):
    return [p if k == 0 else swap(p, axis, k) for k, p in enumerate(pieces)]


def sum_all(x, axis):
    if lax.axis_size(axis) > 8:
        return lax.psum(x, axis)
    bit = 1
    while bit < lax.axis_size(axis):
        x = x + swap(x, axis, bit)
        bit *= 2
    return x


def bit_of(me, bit):
    return (me & bit) // bit


def reduce_halves(keep, sent, axis, bits):
    me = lax.axis_index(axis)
    x = keep + swap(sent, axis, bits[0]).astype(jnp.float32)
    for bit in bits[1:]:
        half = x.shape[0] // 2
        high = bit_of(me, bit)
        sent = lax.dynamic_slice_in_dim(x, (1 - high) * half, half, 0).astype(jnp.bfloat16)
        x = lax.dynamic_slice_in_dim(x, high * half, half, 0) + swap(sent, axis, bit).astype(jnp.float32)
    return lax.optimization_barrier(x.astype(jnp.bfloat16))


def gather_halves(x, axis, bits):
    me = lax.axis_index(axis)
    for bit in reversed(bits[1:]):
        high = bit_of(me, bit)
        other = swap(x, axis, bit)
        x = jnp.concatenate([jnp.where(high == 0, x, other), jnp.where(high == 0, other, x)], axis=0)
    return x, swap(x, axis, bits[0])


def on_device(
    inputs,
    cotangent,
    expert_id,
    slot_index,
    bucket_ids,
    attention_gain,
    query_weight,
    key_weight,
    value_weight,
    output_weight,
    bias_table,
    expert_gain,
    router_weight,
    expert_in,
    expert_out,
):
    bf16, f32 = jnp.bfloat16, jnp.float32
    length, width = inputs.shape
    buckets, heads = bias_table.shape
    hd = query_weight.shape[1]
    head_size = hd // heads
    experts = router_weight.shape[1]
    expert_devices = lax.axis_size("expert")
    shards = lax.axis_size("shard")
    me_e = lax.axis_index("expert")
    me_s = lax.axis_index("shard")
    part = max(1, 3 * length // (2 * experts * shards))
    owned = -(-(length + experts * (shards - 1)) // (16 * shards)) * 16
    relative = expert_devices <= 8
    w_in, w_out = expert_in[0], expert_out[0]

    sizes = [part] * expert_devices if relative else [expert_devices * part]

    def exchange_experts(pieces):
        if relative:
            return exchange_relative(pieces, "expert")
        blocks = pieces[0].reshape(expert_devices, part, width)
        return [lax.all_to_all(blocks, "expert", 0, 0).reshape(expert_devices * part, width)]

    ow_pieces = gather_relative(output_weight)
    far_in, far_out = swap(w_in, "shard", 2), swap(w_out, "shard", 2)
    near_in, near_out = swap(w_in, "shard", 1), swap(w_out, "shard", 1)

    residue = slot_index % shards
    group = slot_index // shards
    order = jnp.arange(length, dtype=jnp.int32)
    earlier = (order[None, :] < order[:, None]) & (residue[None, :] == residue[:, None])
    rank = jnp.sum(earlier.astype(jnp.int32), axis=1)
    place = (residue ^ me_s) * owned + rank
    numbers = jnp.arange(shards * owned, dtype=jnp.int32)[:, None]
    perm_flag = numbers == place[None, :]
    perm = perm_flag.astype(bf16)
    perm_absolute = (numbers == (residue * owned + rank)[None, :]).astype(bf16)
    own_flag = perm_flag[:owned]
    own = perm[:owned]

    def packing(expert):
        target = jnp.where(group < part, expert * part + group, -1)
        target_own = jnp.sum(jnp.where(own_flag, target[None, :] + 1, 0), axis=1) - 1
        numbers_own = jnp.arange(experts * part, dtype=jnp.int32)
        return (
            (numbers_own[:, None] == target_own[None, :]).astype(bf16),
            (numbers_own[None, :] == target_own[:, None]).astype(bf16),
        )

    pack, pack_t = packing(expert_id ^ me_e if relative else expert_id)
    expert_own = jnp.sum(jnp.where(own_flag, expert_id[None, :], 0), axis=1)

    offsets = jnp.concatenate([bucket_ids[1:, 0][::-1], bucket_ids[0, :], jnp.full((1,), -1, jnp.int32)])
    bucket_flag = offsets[None, :] == jnp.arange(buckets, dtype=jnp.int32)[:, None]
    bias_values = jnp.sum(jnp.where(bucket_flag[None], bias_table.T[:, :, None], 0.0), axis=1)
    mixed_t, qkv_t, normed = attention_forward(
        inputs, attention_gain[None, :], query_weight, key_weight, value_weight, bias_values, heads, head_size
    )
    mixed_t, cotangent, near_in, near_out, *ow_pieces = lax.optimization_barrier(
        (mixed_t, cotangent, near_in, near_out, *ow_pieces)
    )
    mixed = dot(perm, mixed_t, 1, 1).astype(bf16)
    mixed_own = exchange_relative([mixed[k * owned : (k + 1) * owned] for k in range(shards)], "shard")
    source_own = dot(own, inputs)
    grad_own = dot(own, cotangent).astype(bf16)
    grad_sent = dot(packing(expert_id)[0], grad_own).astype(bf16).reshape(expert_devices, part, width)
    grad_rows = lax.all_to_all(grad_sent, "expert", 0, 0)
    if relative:
        grad_rows = jnp.concatenate([lax.dynamic_index_in_dim(grad_rows, me_e ^ k, 0) for k in range(expert_devices)])
    grad_rows = grad_rows.reshape(expert_devices * part, width)

    middle, routed, probability, *pieces = route_tokens(
        mixed_own, ow_pieces, source_own, pack, expert_gain[None, :], router_weight, sizes
    )
    pieces = exchange_experts(pieces)
    pieces[-1], far_in, far_out = lax.optimization_barrier((pieces[-1], far_in, far_out))
    in_all = (w_in, near_in, far_in, swap(far_in, "shard", 1))
    out_all = (w_out, near_out, far_out, swap(far_out, "shard", 1))

    mine = (jnp.arange(experts, dtype=jnp.int32)[None, :] == me_e).astype(f32)
    slope, both, *outcome = expert_forward(pieces, grad_rows, router_weight, mine, in_all, out_all)
    back_rows = exchange_experts(outcome)
    back_grads = exchange_experts(list(expert_backward(both, slope, in_all, out_all, sizes)))
    both_all = lax.all_gather(both, "shard", axis=0, tiled=True)

    chosen = (expert_own[:, None] == jnp.arange(experts, dtype=jnp.int32)[None, :]).astype(f32)
    token_values, router_part, expert_gain_part, *mixed_grad = token_grads(
        back_rows, back_grads, pack_t, middle, routed, probability, chosen, grad_own, expert_gain[None, :],
        router_weight, ow_pieces,
    )
    mixed_grad = jnp.concatenate(exchange_relative(mixed_grad, "shard"), axis=0)
    mixed_grad_t = dot(mixed_grad, perm, 0, 0).astype(bf16)
    token_values = lax.all_gather(token_values, "shard", axis=0, tiled=True)

    w_heads = jnp.stack([w.reshape(width, heads, head_size) for w in (query_weight, key_weight, value_weight)], axis=2)
    w_heads = w_heads.reshape(width, 3 * hd)
    split = (heads - 1) * 3 * head_size
    w_first, w_last = w_heads[:, :split], w_heads[:, split:]
    head_grads, diagonals = [], []
    for h in range(heads):
        head_grad, diagonal = attention_backward(qkv_t, bias_values, mixed_grad_t, h, heads, head_size)
        head_grads.append(head_grad)
        diagonals.append(diagonal)
    bits = [1 << i for i in range(expert_devices.bit_length() - 1)]
    bits_first, bits_last = bits, [*bits[1:2], *bits[:1], *bits[2:]]
    high_first, high_last = bit_of(me_e, bits_first[0]).reshape(1), bit_of(me_e, bits_last[0]).reshape(1)
    keep_first, sent_first, gain_first = first_parts(normed, head_grads[:-1], w_first, high_first)
    qkv_grad_t = jnp.concatenate(head_grads, axis=0)

    normed_part = dot(qkv_grad_t, w_heads, 0, 1)
    half = length // 2
    low = me_s % 2
    other_half = lax.dynamic_slice_in_dim(normed_part, (1 - low) * half, half, 0)
    own_half = lax.dynamic_slice_in_dim(normed_part, low * half, half, 0)
    normed_grad = own_half + swap(other_half.astype(bf16), "shard", 1).astype(f32)
    bit = 2
    while bit < shards:
        sent = lax.optimization_barrier(normed_grad.astype(bf16))
        normed_grad = sent.astype(f32) + swap(sent, "shard", bit).astype(f32)
        bit *= 2

    middle_grad_all = lax.optimization_barrier(dot(perm_absolute, token_values[:, width:], 0, 0).astype(bf16))
    table_part = jnp.sum(jnp.where(bucket_flag[None], jnp.stack(diagonals), 0.0), axis=2).reshape(-1, 1)
    table_part = jnp.pad(table_part, ((0, width - table_part.shape[0]), (0, 0)))
    small = jnp.concatenate([jnp.zeros_like(table_part), expert_gain_part.T, router_part, table_part], axis=1)
    small = jnp.pad(small, ((0, 0), (0, -small.shape[1] % 128)))
    keep_last, sent_last = last_parts(
        normed, head_grads[-1], w_last, gain_first, attention_gain[:, None], middle_grad_all, mixed_t, small, high_last
    )
    if relative:
        block_first = reduce_halves(keep_first, sent_first, "expert", bits_first)
        block_last = reduce_halves(keep_last, sent_last, "expert", bits_last)
        first = gather_halves(block_first, "expert", bits_first)
        last = gather_halves(block_last, "expert", bits_last)
    else:
        whole = []
        for keep, sent, high in ((keep_first, sent_first, high_first), (keep_last, sent_last, high_last)):
            sent = sent.astype(f32)
            low_part, high_part = jnp.where(high == 0, keep, sent), jnp.where(high == 0, sent, keep)
            low_part, high_part = lax.psum((low_part, high_part), "expert")
            whole.append((jnp.where(high == 0, low_part, high_part), jnp.where(high == 0, high_part, low_part)))
        first, last = whole
    both_all, keep_last = lax.optimization_barrier((both_all, keep_last))
    in_gradient, out_gradient = expert_weights(both_all, w_in, w_out, shards)
    query_gradient, key_gradient, value_gradient, output_gradient, small = place_sums(
        first, last, high_first, high_last, heads, head_size
    )
    table_gradient = small[: buckets * heads, 2 + experts].reshape(heads, buckets).T
    small = sum_all(small[:, : 2 + experts].T, "shard")

    result = dot(perm_absolute, token_values[:, :width], 0, 0).astype(bf16)
    source_half = lax.dynamic_slice_in_dim(inputs, low * half, half, 0).astype(f32)
    inverse_half = lax.rsqrt(jnp.mean(source_half * source_half, axis=-1, keepdims=True) + 1e-06)
    middle_half = lax.dynamic_slice_in_dim(middle_grad_all, low * half, half, 0).astype(f32)
    w = normed_grad * attention_gain
    grad_half = middle_half + inverse_half * w - source_half * (
        inverse_half * inverse_half * inverse_half * jnp.mean(w * source_half, axis=-1, keepdims=True)
    )
    grad_other = swap(grad_half, "shard", 1)
    input_gradient = jnp.concatenate(
        [jnp.where(low == 0, grad_half, grad_other), jnp.where(low == 0, grad_other, grad_half)], axis=0
    )
    return (
        result,
        input_gradient,
        small[0],
        query_gradient,
        key_gradient,
        value_gradient,
        output_gradient,
        table_gradient,
        small[1],
        small[2:].T,
        in_gradient[None],
        out_gradient[None],
    )


def solution(mesh):
    placed = (
        P("expert", None),
        P("expert", None),
        P("expert"),
        P("expert"),
        P(),
        P(),
        P(None, "shard"),
        P(None, "shard"),
        P(None, "shard"),
        P("shard", None),
        P(None, "shard"),
        P(),
        P(),
        P("expert", None, "shard"),
        P("expert", "shard", None),
    )
    return jax.shard_map(
        on_device,
        mesh=mesh,
        in_specs=placed,
        out_specs=(
            P("expert", None),
            P("expert", None),
            P(),
            P(None, "shard"),
            P(None, "shard"),
            P(None, "shard"),
            P("shard", None),
            P(None, "shard"),
            P(),
            P(),
            P("expert", None, "shard"),
            P("expert", "shard", None),
        ),
        check_vma=False,
    )
```

```python
import functools
import jax
import jax.numpy as jnp
from jax import lax
from jax.experimental import pallas as pl
from jax.experimental.pallas import tpu as pltpu
from jax.sharding import PartitionSpec as P

TIMES = {"attention_forward": 9.4, "attention_backward": 6.7, "route_tokens": 4.7, "expert_near": 8.4, "expert_far": 9.6, "token_grads": 5.0, "first_parts": 8.0, "last_parts": 3.2, "place_sums": 2.9, "place_halves": 3.8, "expert_weights": 14.3, "place_grads": 3.4}


def cost(name):
    return pl.CostEstimate(flops=int(TIMES[name] * 1.15e9), bytes_accessed=10**5, transcendentals=0)


VMEM_LIMIT = 56 * 1024 * 1024


def dot(a, b, ca=1, cb=0):
    return lax.dot_general(a, b, (((ca,), (cb,)), ((), ())), preferred_element_type=jnp.float32)


def bias_strip(values_row, rows):
    total = values_row.shape[-1]
    wide = jnp.broadcast_to(values_row.reshape(1, total), (rows, total))
    return pltpu.roll(wide, total - rows + 1, 1, stride=1, stride_axis=0)


def attention_forward_kernel(heads, head_size, rows, in_ref, gain_ref, wq_ref, wk_ref, wv_ref, bias_ref, mixed_ref, qkv_ref, normed_ref, strip_ref):
    length = in_ref.shape[0]
    blocks = length // rows
    hd = heads * head_size
    source = in_ref[...].astype(jnp.float32)
    inverse = lax.rsqrt(jnp.mean(source * source, axis=1, keepdims=True) + 1e-06)
    normed_ref[...] = (source * inverse * gain_ref[...]).astype(jnp.bfloat16)
    for at, ref in enumerate((wq_ref, wk_ref, wv_ref)):
        qkv_ref[at * hd : (at + 1) * hd, :] = dot(ref[...], normed_ref[...], 1, 1).astype(jnp.bfloat16)
    for h in range(heads):
        strip_ref[...] = bias_strip(bias_ref[h : h + 1, :], rows)
        q = (qkv_ref[h * head_size : (h + 1) * head_size, :].astype(jnp.float32) * 0.125).T.astype(jnp.bfloat16)
        kt = qkv_ref[hd + h * head_size : hd + (h + 1) * head_size, :]
        vt = qkv_ref[2 * hd + h * head_size : 2 * hd + (h + 1) * head_size, :]
        for i in range(blocks):
            s = dot(q[i * rows : (i + 1) * rows], kt)
            at = (blocks - 1 - i) * rows
            s = s + strip_ref[:, at : at + length]
            peak = jnp.max(s, axis=1, keepdims=True)
            p = jnp.exp(s - peak)
            total = jnp.sum(p, axis=1, keepdims=True)
            o = dot(p.astype(jnp.bfloat16), vt, 1, 1) / total
            mixed_ref[h * head_size : (h + 1) * head_size, i * rows : (i + 1) * rows] = o.T.astype(jnp.bfloat16)


def in_vmem(count):
    return [pl.BlockSpec(memory_space=pltpu.VMEM)] * count


def attention_forward(inputs, gain, wq, wk, wv, bias_values, heads, head_size, rows=256):
    length = inputs.shape[0]
    hd = heads * head_size
    return pl.pallas_call(
        functools.partial(attention_forward_kernel, heads, head_size, rows),
        out_shape=(
            jax.ShapeDtypeStruct((hd, length), jnp.bfloat16),
            jax.ShapeDtypeStruct((3 * hd, length), jnp.bfloat16),
            jax.ShapeDtypeStruct(inputs.shape, jnp.bfloat16),
        ),
        in_specs=in_vmem(6),
        out_specs=tuple(in_vmem(3)),
        scratch_shapes=[pltpu.VMEM((rows, bias_values.shape[1]), jnp.float32)],
        compiler_params=pltpu.CompilerParams(vmem_limit_bytes=VMEM_LIMIT),
        cost_estimate=cost("attention_forward"),
        name="attention_forward",
    )(inputs, gain, wq, wk, wv, bias_values)


def call(body, out_shape, args, name, flops, scratch=(), transcendentals=0):
    return pl.pallas_call(
        body,
        out_shape=out_shape,
        in_specs=in_vmem(len(args)),
        out_specs=jax.tree.map(lambda _: in_vmem(1)[0], out_shape),
        scratch_shapes=list(scratch),
        compiler_params=pltpu.CompilerParams(vmem_limit_bytes=VMEM_LIMIT),
        cost_estimate=cost(name),
        name=name,
    )(*args)


def shape(dims, dtype=jnp.bfloat16):
    return jax.ShapeDtypeStruct(dims, dtype)


def join(refs, target):
    at = 0
    for ref in refs:
        target[at : at + ref.shape[0], :] = ref[...]
        at += ref.shape[0]


def route_tokens(mixed_pieces, ow_pieces, source, grad, pack, gain, router, sizes):
    shards = len(mixed_pieces)
    tokens, width = source.shape

    def body(*refs):
        mixed_refs, ow_refs = refs[:shards], refs[shards : 2 * shards]
        source_ref, grad_ref, pack_ref, gain_ref, router_ref = refs[2 * shards : 2 * shards + 5]
        middle_ref, routed_ref, probability_ref = refs[2 * shards + 5 : 2 * shards + 8]
        middle = source_ref[...]
        for m, o in zip(mixed_refs, ow_refs):
            middle = middle + dot(m[...], o[...])
        middle_ref[...] = middle
        spread = lax.rsqrt(jnp.mean(middle * middle, axis=1, keepdims=True) + 1e-06)
        routed = (middle * spread * gain_ref[...]).astype(jnp.bfloat16)
        routed_ref[...] = routed
        packed = dot(pack_ref[...], routed).astype(jnp.bfloat16)
        packed_grad = dot(pack_ref[...], grad_ref[...]).astype(jnp.bfloat16)
        at = 0
        for ref in refs[2 * shards + 8 :]:
            size = ref.shape[0] // 2
            ref[:size, :] = packed[at : at + size, :]
            ref[size:, :] = packed_grad[at : at + size, :]
            at += size
        logits = dot(routed, router_ref[...], 1, 1)
        powered = jnp.exp(logits - jnp.max(logits, axis=1, keepdims=True))
        probability_ref[...] = powered / jnp.sum(powered, axis=1, keepdims=True)

    out = (shape((tokens, width), jnp.float32), shape((tokens, width)), shape((tokens, router.shape[0]), jnp.float32))
    out = out + tuple(shape((2 * n, width)) for n in sizes)
    args = (*mixed_pieces, *ow_pieces, source, grad, pack, gain, router)
    return call(body, out, args, "route_tokens", 0)


def gated(rows, grads, router, mine):
    logits = dot(rows, router, 1, 1)
    powered = jnp.exp(logits - jnp.max(logits, axis=1, keepdims=True))
    gate = jnp.sum(powered * mine, axis=1, keepdims=True) / jnp.sum(powered, axis=1, keepdims=True)
    return (gate * grads.astype(jnp.float32)).astype(jnp.bfloat16)


def expert_units(rows, grads, in_parts, out, out_ref, grad_ref):
    at, before = 0, 0.0
    for part in in_parts:
        before = before + dot(rows[:, at : at + part.shape[0]], part)
        at += part.shape[0]
    value, slope = gelu_pair(before)
    out_ref[...] += dot(value.astype(jnp.bfloat16), out)
    before_grad = (dot(grads, out, 1, 1) * slope).astype(jnp.bfloat16)
    at = 0
    for part in in_parts:
        grad_ref[:, at : at + part.shape[0]] += dot(before_grad, part, 1, 1)
        at += part.shape[0]


def expert_near(pieces, router, mine, weights, part):
    count, width = part * len(pieces), pieces[0].shape[1]
    n = len(pieces)

    def body(*refs):
        router_ref, mine_ref, in0, out0, in1, out1, both_ref, out_ref, grad_ref = refs[n:]
        for i, ref in enumerate(refs[:n]):
            both_ref[i * part : (i + 1) * part, :] = ref[:part, :]
            both_ref[count + i * part : count + (i + 1) * part, :] = ref[part:, :]
        rows = both_ref[:count, :]
        both_ref[count:, :] = gated(rows, both_ref[count:, :], router_ref[...], mine_ref[...])
        out_ref[...] = jnp.zeros_like(out_ref)
        grad_ref[...] = jnp.zeros_like(grad_ref)
        for i, o in ((in0, out0), (in1, out1)):
            expert_units(rows, both_ref[count:, :], (i[...],), o[...], out_ref, grad_ref)

    out = (shape((2 * count, width)), shape((count, width), jnp.float32), shape((count, width), jnp.float32))
    return call(body, out, (*pieces, router, mine, *weights), "expert_near", 0)


def expert_far(both, out_before, grad_before, weights, part):
    count, width = out_before.shape

    def body(both_ref, out_ref, grad_ref, in0, out0, in1, out1, *refs):
        out_total, grad_total = refs[-2:]
        out_total[...] = out_ref[...]
        grad_total[...] = grad_ref[...]
        for i, o in ((in0, out0), (in1, out1)):
            expert_units(both_ref[:count, :], both_ref[count:, :], (i[...],), o[...], out_total, grad_total)
        for i, ref in enumerate(refs[:-2]):
            ref[:part, :] = out_total[i * part : (i + 1) * part, :].astype(jnp.bfloat16)
            ref[part:, :] = grad_total[i * part : (i + 1) * part, :].astype(jnp.bfloat16)

    out = tuple(shape((2 * part, width)) for _ in range(count // part))
    scratch = [pltpu.VMEM((count, width), jnp.float32)] * 2
    return list(call(body, out, (both, out_before, grad_before, *weights), "expert_far", 0, scratch))


def token_grads(back, pack_t, middle, routed, probability, chosen, grad, gain, router, ow_pieces):
    tokens, width = middle.shape
    n, shards = len(back), len(ow_pieces)
    hd = ow_pieces[0].shape[0]

    def body(*refs):
        pack_ref, middle_ref, routed_ref, probability_ref, chosen_ref, g_ref, gain_ref, router_ref = refs[n : n + 8]
        ow_refs = refs[n + 8 : n + 8 + shards]
        result_ref, grad_out_ref, router_part_ref, gain_part_ref = refs[n + 8 + shards : n + 12 + shards]
        mixed_refs = refs[n + 12 + shards : n + 12 + 2 * shards]
        buffer = refs[-1]
        g = g_ref[...].astype(jnp.float32)
        middle = middle_ref[...]
        chosen = chosen_ref[...]
        probability = probability_ref[...]
        gate = jnp.sum(probability * chosen, axis=1, keepdims=True)
        half = buffer.shape[0] // n
        for i, ref in enumerate(refs[:n]):
            buffer[i * half : (i + 1) * half, :] = ref[:half, :]
        rows = dot(pack_ref[...], buffer[...])
        result_ref[...] = (middle + gate * rows).astype(jnp.bfloat16)
        gate_grad = jnp.sum(g * rows, axis=1, keepdims=True)
        logit_grad = (gate_grad * gate * (chosen - probability)).astype(jnp.bfloat16)
        router_part_ref[...] = dot(logit_grad, routed_ref[...], 0, 0)
        for i, ref in enumerate(refs[:n]):
            buffer[i * half : (i + 1) * half, :] = ref[half:, :]
        routed_grad = dot(logit_grad, router_ref[...]) + dot(pack_ref[...], buffer[...])
        spread = lax.rsqrt(jnp.mean(middle * middle, axis=1, keepdims=True) + 1e-06)
        gain_part_ref[...] = jnp.sum(routed_grad * middle * spread, axis=0, keepdims=True)
        u = routed_grad * gain_ref[...]
        mean = jnp.mean(u * middle, axis=1, keepdims=True)
        middle_grad = (g + spread * u - middle * (spread * spread * spread * mean)).astype(jnp.bfloat16)
        grad_out_ref[...] = middle_grad
        for m, o in zip(mixed_refs, ow_refs):
            m[...] = dot(middle_grad, o[...], 1, 1).astype(jnp.bfloat16)

    out = (
        shape((tokens, width)),
        shape((tokens, width)),
        shape(router.shape, jnp.float32),
        shape((1, width), jnp.float32),
    ) + (shape((tokens, hd)),) * shards
    args = (*back, pack_t, middle, routed, probability, chosen, grad, gain, router, *ow_pieces)
    scratch = [pltpu.VMEM((pack_t.shape[1], width), jnp.bfloat16)]
    return call(body, out, args, "token_grads", 0, scratch)


def cut_halves(part, bit, keep_ref, sent_ref):
    half = keep_ref.shape[0]
    keep_ref[...] = part[pl.ds(pl.multiple_of(bit * half, half), half), :]
    sent_ref[...] = part[pl.ds(pl.multiple_of((1 - bit) * half, half), half), :].astype(jnp.bfloat16)


def weight_part(head_ref, normed_ref, weight_refs, h, part, at):
    value = dot(head_ref[...], normed_ref[...])
    part[at : at + value.shape[0], :] = value
    size = value.shape[0] // 3
    gain = jnp.zeros((1, value.shape[1]), jnp.float32)
    for c, ref in enumerate(weight_refs):
        weight = ref[h * size : (h + 1) * size, :].astype(jnp.float32)
        gain = gain + jnp.sum(weight * value[c * size : (c + 1) * size, :], axis=0, keepdims=True)
    return gain


def place_grads(pieces, perm):
    tokens, hd = pieces[0].shape
    n = len(pieces)

    def body(*refs):
        perm_ref, out_ref = refs[n : n + 2]
        buffer = refs[-1]
        join(refs[:n], buffer)
        out_ref[...] = dot(buffer[...], perm_ref[...], 0, 0).astype(jnp.bfloat16)

    scratch = [pltpu.VMEM((n * tokens, hd), jnp.bfloat16)]
    return call(body, shape((hd, perm.shape[1])), (*pieces, perm), "place_grads", 0, scratch)


def first_parts(normed, head_grads, weights, middle_pieces, back, mixed_t, high):
    width = normed.shape[1]
    rows = head_grads[0].shape[0]
    n, hd = len(head_grads), mixed_t.shape[0]
    total = rows * n + hd

    def body(high_ref, normed_ref, wq_ref, wk_ref, wv_ref, back_ref, mixed_ref, *refs):
        keep_ref, sent_ref, gain_ref, middle_ref, part, buffer = refs[n + len(middle_pieces) :]
        gain = jnp.zeros(gain_ref.shape, jnp.float32)
        for h, ref in enumerate(refs[:n]):
            gain = gain + weight_part(ref, normed_ref, (wq_ref, wk_ref, wv_ref), h, part, h * rows)
        gain_ref[...] = gain
        join(refs[n : n + len(middle_pieces)], buffer)
        middle_ref[...] = dot(back_ref[...], buffer[...]).astype(jnp.bfloat16)
        part[n * rows :, :] = dot(mixed_ref[...], middle_ref[...])
        cut_halves(part, high_ref[0], keep_ref, sent_ref)

    out = (
        shape((total // 2, width), jnp.float32),
        shape((total // 2, width)),
        shape((1, width), jnp.float32),
        shape(normed.shape),
    )
    args = (normed, *weights, back, mixed_t, *head_grads, *middle_pieces)
    scratch = [pltpu.VMEM((total, width), jnp.float32), pltpu.VMEM((back.shape[1], width), jnp.bfloat16)]
    return with_bit(body, out, args, high, "first_parts", scratch)


def with_bit(body, out, args, high, name, scratch=()):
    return pl.pallas_call(
        body,
        out_shape=out,
        in_specs=[pl.BlockSpec(memory_space=pltpu.SMEM)] + in_vmem(len(args)),
        out_specs=jax.tree.map(lambda _: in_vmem(1)[0], out),
        scratch_shapes=list(scratch),
        compiler_params=pltpu.CompilerParams(vmem_limit_bytes=VMEM_LIMIT),
        cost_estimate=cost(name),
        name=name,
    )(high, *args)


def last_parts(normed, head_grad, weights, h, gain_before, gain, small, high):
    width = normed.shape[1]
    rows = head_grad.shape[0]
    total = rows + small.shape[0]

    def body(high_ref, normed_ref, head_ref, wq_ref, wk_ref, wv_ref, before_ref, gain_ref, small_ref, *refs):
        keep_ref, sent_ref, part = refs
        gain_part = weight_part(head_ref, normed_ref, (wq_ref, wk_ref, wv_ref), h, part, 0)
        line = lax.broadcasted_iota(jnp.int32, small_ref.shape, 0)
        gain_part = (before_ref[...] + gain_part) / gain_ref[...]
        part[rows:, :] = jnp.where(line == 0, gain_part, small_ref[...])
        cut_halves(part, high_ref[0], keep_ref, sent_ref)

    out = (shape((total // 2, width), jnp.float32), shape((total // 2, width)))
    args = (normed, head_grad, *weights, gain_before, gain, small)
    return with_bit(body, out, args, high, "last_parts", [pltpu.VMEM((total, width), jnp.float32)])


def place_sums(first, last, bits, heads, head_size):
    width = first[0].shape[1]
    hd = heads * head_size
    totals = (2 * first[0].shape[0], 2 * last[0].shape[0])

    def body(bits_ref, a0, a1, b0, b1, q_ref, k_ref, v_ref, o_ref, small_ref, first_sum, last_sum):
        for i, (own, other, target) in enumerate(((a0, a1, first_sum), (b0, b1, last_sum))):
            half = own.shape[0]
            target[pl.ds(pl.multiple_of(bits_ref[i] * half, half), half), :] = own[...].astype(jnp.float32)
            target[pl.ds(pl.multiple_of((1 - bits_ref[i]) * half, half), half), :] = other[...].astype(jnp.float32)
        for h in range(heads):
            source, at = (first_sum, 3 * h * head_size) if h < heads - 1 else (last_sum, 0)
            for c, ref in enumerate((q_ref, k_ref, v_ref)):
                start = at + c * head_size
                ref[h * head_size : (h + 1) * head_size, :] = source[start : start + head_size, :]
        o_ref[...] = first_sum[3 * (heads - 1) * head_size :, :]
        small_ref[...] = last_sum[3 * head_size :, :]

    out = (shape((hd, width), jnp.float32),) * 4 + (shape((totals[1] - 3 * head_size, width), jnp.float32),)
    scratch = [pltpu.VMEM((total, width), jnp.float32) for total in totals]
    return with_bit(body, out, (*first, *last), bits, "place_sums", scratch)


def place_halves(own, other, low):
    half, width = own.shape

    def body(low_ref, own_ref, other_ref, out_ref):
        out_ref[pl.ds(pl.multiple_of(low_ref[0] * half, half), half), :] = own_ref[...]
        out_ref[pl.ds(pl.multiple_of((1 - low_ref[0]) * half, half), half), :] = other_ref[...]

    return with_bit(body, shape((2 * half, width), own.dtype), (own, other), low.reshape(1), "place_halves")


def expert_weights(both_all, w_in, w_out):
    shards, _, count, width = both_all.shape

    def body(both_ref, wi_ref, wo_ref, in_ref, out_ref):
        for s in range(shards):
            rows, grads = both_ref[s, 0], both_ref[s, 1]
            value, slope = gelu_pair(dot(rows, wi_ref[...]))
            before_grad = (dot(grads, wo_ref[...], 1, 1) * slope).astype(jnp.bfloat16)
            part_in = dot(rows, before_grad, 0, 0)
            part_out = dot(value.astype(jnp.bfloat16), grads, 0, 0)
            if s == 0:
                in_ref[...] = part_in
                out_ref[...] = part_out
            else:
                in_ref[...] += part_in
                out_ref[...] += part_out

    out = (shape(w_in.shape, jnp.float32), shape(w_out.shape, jnp.float32))
    return call(body, out, (both_all, w_in, w_out), "expert_weights", 10**10)


def attention_backward_kernel(h, heads, head_size, rows, qkv_ref, bias_ref, grad_ref, out_ref, diag_ref, strip_ref, total_ref):
    length = qkv_ref.shape[1]
    blocks = length // rows
    hd = heads * head_size
    width = bias_ref.shape[1]
    strip_ref[...] = bias_strip(bias_ref[h : h + 1, :], rows)
    total_ref[...] = jnp.zeros_like(total_ref)
    qt32 = qkv_ref[h * head_size : (h + 1) * head_size, :].astype(jnp.float32) * 0.125
    qt = qt32.astype(jnp.bfloat16)
    q = qt32.T.astype(jnp.bfloat16)
    kt = qkv_ref[hd + h * head_size : hd + (h + 1) * head_size, :]
    k = kt.astype(jnp.float32).T.astype(jnp.bfloat16)
    vt = qkv_ref[2 * hd + h * head_size : 2 * hd + (h + 1) * head_size, :]
    gt = grad_ref[h * head_size : (h + 1) * head_size, :]
    g = gt.astype(jnp.float32).T.astype(jnp.bfloat16)
    dk = jnp.zeros((head_size, length), jnp.float32)
    dv = jnp.zeros((head_size, length), jnp.float32)
    for i in range(blocks):
        at = (blocks - 1 - i) * rows
        part = slice(i * rows, (i + 1) * rows)
        s = dot(q[part], kt) + strip_ref[:, at : at + length]
        peak = jnp.max(s, axis=1, keepdims=True)
        p = jnp.exp(s - peak)
        p = p * (1.0 / jnp.sum(p, axis=1, keepdims=True))
        dp = dot(g[part], vt)
        delta = jnp.sum(p * dp, axis=1, keepdims=True)
        ds = p * (dp - delta)
        total_ref[:, at : at + length] += ds
        dsb = ds.astype(jnp.bfloat16)
        dv = dv + dot(gt[:, part], p.astype(jnp.bfloat16))
        dk = dk + dot(qt[:, part], dsb)
        dq = dot(dsb, k) * 0.125
        out_ref[0:head_size, part] = dq.T.astype(jnp.bfloat16)
    out_ref[head_size : 2 * head_size, :] = dk.astype(jnp.bfloat16)
    out_ref[2 * head_size : 3 * head_size, :] = dv.astype(jnp.bfloat16)
    folded = total_ref[...]
    half = rows // 2
    while half:
        folded = folded[:half] + pltpu.roll(folded[half:], width - half, 1)
        half //= 2
    diag_ref[...] = pltpu.roll(folded, rows - 1, 1)


def attention_backward(qkv_t, bias_values, grad_t, h, heads, head_size, rows=256):
    length = qkv_t.shape[1]
    width = bias_values.shape[1]
    return pl.pallas_call(
        functools.partial(attention_backward_kernel, h, heads, head_size, rows),
        out_shape=(jax.ShapeDtypeStruct((3 * head_size, length), jnp.bfloat16), jax.ShapeDtypeStruct((1, width), jnp.float32)),
        in_specs=[pl.BlockSpec(memory_space=pltpu.VMEM)] * 3,
        out_specs=(pl.BlockSpec(memory_space=pltpu.VMEM),) * 2,
        scratch_shapes=[pltpu.VMEM((rows, width), jnp.float32)] * 2,
        compiler_params=pltpu.CompilerParams(vmem_limit_bytes=VMEM_LIMIT),
        cost_estimate=cost("attention_backward"),
        name="attention_backward",
    )(qkv_t, bias_values, grad_t)


def gelu_pair(v):
    inner = 0.7978845608028654 * (v + 0.044715 * v * v * v)
    t = jnp.tanh(inner)
    slope = 0.7978845608028654 * (1.0 + 3.0 * 0.044715 * v * v)
    return 0.5 * v * (1.0 + t), 0.5 * (1.0 + t) + 0.5 * v * (1.0 - t * t) * slope


def swap(x, axis, k):
    return lax.ppermute(x, axis, [(i, i ^ k) for i in range(lax.axis_size(axis))])


def gather_relative(x, axis="shard"):
    pieces = {0: x}
    bit = lax.axis_size(axis) // 2
    while bit:
        for k in sorted(pieces):
            pieces[k ^ bit] = swap(pieces[k], axis, bit)
        bit //= 2
    return [pieces[k] for k in range(len(pieces))]


def exchange_relative(pieces, axis):
    return [p if k == 0 else swap(p, axis, k) for k, p in enumerate(pieces)]


def exchange_window(pieces, axis, window):
    received = [pieces[0]]
    for k in range(1, len(pieces)):
        sent = pieces[k]
        if k > window:
            sent, received[k - window] = lax.optimization_barrier((sent, received[k - window]))
        received.append(swap(sent, axis, k))
    return received


def sum_pairs(x, axis):
    if lax.axis_size(axis) != 4:
        return lax.psum(x, axis)
    one, two, three = (swap(x, axis, k) for k in (1, 2, 3))
    return (x + one) + (two + three)


def sum_all(x, axis):
    if lax.axis_size(axis) > 8:
        return lax.psum(x, axis)
    bit = 1
    while bit < lax.axis_size(axis):
        x = x + swap(x, axis, bit)
        bit *= 2
    return x


def bit_of(me, bit):
    return (me & bit) // bit


def reduce_halves(keep, received, axis, bits, beside=None):
    me = lax.axis_index(axis)
    x = keep + received.astype(jnp.float32)
    for bit in bits[1:]:
        half = x.shape[0] // 2
        high = bit_of(me, bit)
        sent = lax.dynamic_slice_in_dim(x, (1 - high) * half, half, 0).astype(jnp.bfloat16)
        received = swap(sent, axis, bit)
        if bit == bits[1] and beside is not None:
            received, beside = lax.optimization_barrier((received, beside))
        x = lax.dynamic_slice_in_dim(x, high * half, half, 0) + received.astype(jnp.float32)
    return lax.optimization_barrier(x.astype(jnp.bfloat16)), beside


def gather_halves(x, axis, bits):
    me = lax.axis_index(axis)
    for bit in reversed(bits[1:]):
        high = bit_of(me, bit)
        other = swap(x, axis, bit)
        x = jnp.concatenate([jnp.where(high == 0, x, other), jnp.where(high == 0, other, x)], axis=0)
    return x, swap(x, axis, bits[0])


def on_device(
    inputs,
    cotangent,
    expert_id,
    slot_index,
    bucket_ids,
    attention_gain,
    query_weight,
    key_weight,
    value_weight,
    output_weight,
    bias_table,
    expert_gain,
    router_weight,
    expert_in,
    expert_out,
):
    bf16, f32 = jnp.bfloat16, jnp.float32
    length, width = inputs.shape
    buckets, heads = bias_table.shape
    hd = query_weight.shape[1]
    head_size = hd // heads
    experts = router_weight.shape[1]
    expert_devices = lax.axis_size("expert")
    shards = lax.axis_size("shard")
    me_e = lax.axis_index("expert")
    me_s = lax.axis_index("shard")
    part = max(1, 3 * length // (2 * experts * shards))
    owned = -(-(length + experts * (shards - 1)) // (16 * shards)) * 16
    relative = expert_devices <= 8
    w_in, w_out = expert_in[0], expert_out[0]

    sizes = [part] * expert_devices

    def exchange_experts(pieces):
        if relative:
            return exchange_window(pieces, "expert", 4)
        blocks = jnp.stack(pieces)
        return list(lax.all_to_all(blocks, "expert", 0, 0))

    ow_pieces = gather_relative(output_weight)
    far_in = swap(w_in, "shard", 2)

    w_rows = (query_weight.T, key_weight.T, value_weight.T)
    router_rows = router_weight.T

    residue = slot_index % shards
    group = slot_index // shards
    order = jnp.arange(length, dtype=jnp.int32)
    earlier = (order[None, :] < order[:, None]) & (residue[None, :] == residue[:, None])
    rank = jnp.sum(earlier.astype(jnp.int32), axis=1)
    place = (residue ^ me_s) * owned + rank
    numbers = jnp.arange(shards * owned, dtype=jnp.int32)[:, None]
    perm_flag = numbers == place[None, :]
    perm = lax.optimization_barrier(perm_flag.astype(bf16))
    own_flag = perm_flag[:owned]
    own = perm[:owned]

    def packing(expert):
        target = jnp.where(group < part, expert * part + group, -1)
        target_own = jnp.sum(jnp.where(own_flag, target[None, :] + 1, 0), axis=1) - 1
        numbers_own = jnp.arange(experts * part, dtype=jnp.int32)
        return (
            (numbers_own[:, None] == target_own[None, :]).astype(bf16),
            (numbers_own[None, :] == target_own[:, None]).astype(bf16),
        )

    pack, pack_t = packing(expert_id ^ me_e if relative else expert_id)
    expert_own = jnp.sum(jnp.where(own_flag, expert_id[None, :], 0), axis=1)

    offsets = jnp.concatenate([bucket_ids[1:, 0][::-1], bucket_ids[0, :], jnp.full((1,), -1, jnp.int32)])
    bucket_flag = offsets[None, :] == jnp.arange(buckets, dtype=jnp.int32)[:, None]
    bias_values = jnp.sum(jnp.where(bucket_flag[None], bias_table.T[:, :, None], 0.0), axis=1)
    mixed_t, qkv_t, normed = attention_forward(
        inputs, attention_gain[None, :], *w_rows, bias_values, heads, head_size
    )
    mixed_t, *ow_pieces = lax.optimization_barrier((mixed_t, *ow_pieces))
    mixed = dot(perm, mixed_t, 1, 1).astype(bf16)
    place, rank, mixed = lax.optimization_barrier((place, rank, mixed))
    back = lax.optimization_barrier((place[:, None] == numbers.T).astype(bf16))
    back_absolute = lax.optimization_barrier(((residue * owned + rank)[:, None] == numbers.T).astype(bf16))
    mixed_own = exchange_relative([mixed[k * owned : (k + 1) * owned] for k in range(shards)], "shard")
    source_own = dot(own, inputs)
    grad_own = dot(own, cotangent).astype(bf16)

    far_in, near_in, near_out, *mixed_own = lax.optimization_barrier((far_in, w_in, w_out, *mixed_own))
    far_out = swap(near_out, "shard", 2)
    near_in, near_out, last_in = swap(near_in, "shard", 1), swap(near_out, "shard", 1), swap(far_in, "shard", 1)

    middle, routed, probability, *pieces = route_tokens(
        mixed_own, ow_pieces, source_own, grad_own, pack, expert_gain[None, :], router_rows, sizes
    )
    near_in, near_out, last_in, *pieces = lax.optimization_barrier((near_in, near_out, last_in, *pieces))
    pieces = exchange_experts(pieces)
    far_out, *pieces = lax.optimization_barrier((far_out, *pieces))
    last_out = swap(far_out, "shard", 1)

    mine = (jnp.arange(experts, dtype=jnp.int32)[None, :] == me_e).astype(f32)
    both, out_near, grad_near = expert_near(pieces, router_rows, mine, (w_in, w_out, near_in, near_out), part)
    both_all = lax.all_gather(both.reshape(2, expert_devices * part, width), "shard", axis=0)
    out_near, last_out = lax.optimization_barrier((out_near, last_out))
    far_all = (far_in, far_out, last_in, last_out)
    back_pieces = exchange_experts(expert_far(both, out_near, grad_near, far_all, part))

    chosen = (expert_own[:, None] == jnp.arange(experts, dtype=jnp.int32)[None, :]).astype(f32)
    result_own, attention_grad, router_part, expert_gain_part, *mixed_grad = token_grads(
        back_pieces, pack_t, middle, routed, probability, chosen, grad_own, expert_gain[None, :],
        router_rows, ow_pieces,
    )
    mixed_grad = exchange_relative(mixed_grad, "shard")
    in_gradient, out_gradient = expert_weights(both_all, w_in, w_out)
    attention_grad, in_gradient, out_gradient, *mixed_grad = lax.optimization_barrier(
        (attention_grad, in_gradient, out_gradient, *mixed_grad)
    )
    far_grad, near_grad = swap(attention_grad, "shard", 2), swap(attention_grad, "shard", 1)
    mixed_grad_t = place_grads(mixed_grad, perm)
    results = lax.all_gather(result_own, "shard", axis=0, tiled=True)

    w_heads = jnp.concatenate([w[h * head_size : (h + 1) * head_size] for h in range(heads) for w in w_rows], axis=0)
    bits = [1 << i for i in range(expert_devices.bit_length() - 1)]
    bits_first, bits_last = bits, [*bits[1:2], *bits[:1], *bits[2:]]
    high_first, high_last = bit_of(me_e, bits_first[0]).reshape(1), bit_of(me_e, bits_last[0]).reshape(1)
    head_grads, diagonals = [], []
    for h in range(heads):
        if h == heads - 1:
            keep_first, sent_first, gain_first, middle_grad_all = first_parts(
                normed, head_grads, w_rows, attention_grads, back, mixed_t, high_first
            )
            mixed_grad_t, sent_first, middle_grad_all = lax.optimization_barrier(
                (mixed_grad_t, sent_first, middle_grad_all)
            )
        head_grad, diagonal = attention_backward(qkv_t, bias_values, mixed_grad_t, h, heads, head_size)
        if h == 0:
            far_grad, near_grad, head_grad = lax.optimization_barrier((far_grad, near_grad, head_grad))
            attention_grads = [attention_grad, near_grad, far_grad, swap(far_grad, "shard", 1)]
        if h == heads - 1 and relative:
            received, head_grad, diagonal = lax.optimization_barrier(
                (swap(sent_first, "expert", bits_first[0]), head_grad, diagonal)
            )
        head_grads.append(head_grad)
        diagonals.append(diagonal)
    qkv_grad_t = jnp.concatenate(head_grads, axis=0)

    normed_part = dot(qkv_grad_t, w_heads, 0, 0)
    half = length // 2
    low = me_s % 2
    other_half = lax.dynamic_slice_in_dim(normed_part, (1 - low) * half, half, 0)
    own_half = lax.dynamic_slice_in_dim(normed_part, low * half, half, 0)
    near_part = swap(other_half.astype(bf16), "shard", 1)

    table_part = jnp.sum(jnp.where(bucket_flag[None], jnp.stack(diagonals), 0.0), axis=2).reshape(1, -1)
    table_part = jnp.pad(table_part, ((0, 0), (0, width - table_part.shape[1])))
    small = jnp.concatenate([jnp.zeros_like(table_part), expert_gain_part, router_part, table_part], axis=0)
    small = jnp.pad(small, ((0, -small.shape[0] % 64), (0, 0)))
    keep_last, sent_last = last_parts(
        normed, head_grads[-1], w_rows, heads - 1, gain_first, attention_gain[None, :], small, high_last
    )
    if relative:
        block_first, near_part = reduce_halves(keep_first, received, "expert", bits_first, near_part)
        block_last, _ = reduce_halves(keep_last, swap(sent_last, "expert", bits_last[0]), "expert", bits_last)
        near_sum = lax.optimization_barrier((own_half + near_part.astype(f32)).astype(bf16))
        far_sum = swap(near_sum, "shard", 2)
        block_last, far_sum = lax.optimization_barrier((block_last, far_sum))
        first = gather_halves(block_first, "expert", bits_first)
        last = gather_halves(block_last, "expert", bits_last)
    else:
        whole = []
        for keep, sent, high in ((keep_first, sent_first, high_first), (keep_last, sent_last, high_last)):
            sent = sent.astype(f32)
            low_part, high_part = jnp.where(high == 0, keep, sent), jnp.where(high == 0, sent, keep)
            low_part, high_part = lax.psum((low_part, high_part), "expert")
            whole.append((jnp.where(high == 0, low_part, high_part), jnp.where(high == 0, high_part, low_part)))
        first, last = whole
        near_sum = lax.optimization_barrier((own_half + near_part.astype(f32)).astype(bf16))
        far_sum = swap(near_sum, "shard", 2)
    query_gradient, key_gradient, value_gradient, output_gradient, small = place_sums(
        first, last, jnp.concatenate([high_first, high_last]), heads, head_size
    )
    table_gradient = small[2 + experts, : buckets * heads].reshape(heads, buckets).T
    small = sum_pairs(small[: 2 + experts], "shard")

    result = dot(back_absolute, results).astype(bf16)
    normed_grad = near_sum.astype(f32) + far_sum.astype(f32)
    source_half = lax.dynamic_slice_in_dim(inputs, low * half, half, 0).astype(f32)
    inverse_half = lax.rsqrt(jnp.mean(source_half * source_half, axis=-1, keepdims=True) + 1e-06)
    middle_half = lax.dynamic_slice_in_dim(middle_grad_all, low * half, half, 0).astype(f32)
    w = normed_grad * attention_gain
    grad_half = middle_half + inverse_half * w - source_half * (
        inverse_half * inverse_half * inverse_half * jnp.mean(w * source_half, axis=-1, keepdims=True)
    )
    grad_other = swap(grad_half, "shard", 1)
    input_gradient = place_halves(grad_half, grad_other, low)
    return (
        result,
        input_gradient,
        small[0],
        query_gradient.T,
        key_gradient.T,
        value_gradient.T,
        output_gradient,
        table_gradient,
        small[1],
        small[2:].T,
        in_gradient[None],
        out_gradient[None],
    )


def solution(mesh):
    placed = (
        P("expert", None),
        P("expert", None),
        P("expert"),
        P("expert"),
        P(),
        P(),
        P(None, "shard"),
        P(None, "shard"),
        P(None, "shard"),
        P("shard", None),
        P(None, "shard"),
        P(),
        P(),
        P("expert", None, "shard"),
        P("expert", "shard", None),
    )
    return jax.shard_map(
        on_device,
        mesh=mesh,
        in_specs=placed,
        out_specs=(
            P("expert", None),
            P("expert", None),
            P(),
            P(None, "shard"),
            P(None, "shard"),
            P(None, "shard"),
            P("shard", None),
            P(None, "shard"),
            P(),
            P(),
            P("expert", None, "shard"),
            P("expert", "shard", None),
        ),
        check_vma=False,
    )
```

```python
import functools
import jax
import jax.numpy as jnp
from jax import lax
from jax.experimental import pallas as pl
from jax.experimental.pallas import tpu as pltpu
from jax.sharding import PartitionSpec as P

TIMES = {"attention_forward": 9.4, "attention_backward": 6.7, "route_tokens": 4.7, "expert_near": 8.4, "expert_far": 9.6, "token_grads": 5.0, "first_parts": 8.0, "last_parts": 3.2, "place_sums": 2.9, "place_halves": 3.8, "expert_weights": 14.3, "place_grads": 3.4}


def cost(name):
    return pl.CostEstimate(flops=int(TIMES[name] * 1.15e9), bytes_accessed=10**5, transcendentals=0)


VMEM_LIMIT = 56 * 1024 * 1024


def dot(a, b, ca=1, cb=0):
    return lax.dot_general(a, b, (((ca,), (cb,)), ((), ())), preferred_element_type=jnp.float32)


def bias_strip(values_row, rows):
    total = values_row.shape[-1]
    wide = jnp.broadcast_to(values_row.reshape(1, total), (rows, total))
    return pltpu.roll(wide, total - rows + 1, 1, stride=1, stride_axis=0)


def attention_forward_kernel(heads, head_size, rows, in_ref, gain_ref, wq_ref, wk_ref, wv_ref, bias_ref, mixed_ref, qkv_ref, normed_ref, strip_ref):
    length = in_ref.shape[0]
    blocks = length // rows
    hd = heads * head_size
    source = in_ref[...].astype(jnp.float32)
    inverse = lax.rsqrt(jnp.mean(source * source, axis=1, keepdims=True) + 1e-06)
    normed_ref[...] = (source * inverse * gain_ref[...]).astype(jnp.bfloat16)
    for at, ref in enumerate((wq_ref, wk_ref, wv_ref)):
        qkv_ref[at * hd : (at + 1) * hd, :] = dot(ref[...], normed_ref[...], 1, 1).astype(jnp.bfloat16)
    for h in range(heads):
        strip_ref[...] = bias_strip(bias_ref[h : h + 1, :], rows)
        q = (qkv_ref[h * head_size : (h + 1) * head_size, :].astype(jnp.float32) * 0.125).T.astype(jnp.bfloat16)
        kt = qkv_ref[hd + h * head_size : hd + (h + 1) * head_size, :]
        vt = qkv_ref[2 * hd + h * head_size : 2 * hd + (h + 1) * head_size, :]
        for i in range(blocks):
            s = dot(q[i * rows : (i + 1) * rows], kt)
            at = (blocks - 1 - i) * rows
            s = s + strip_ref[:, at : at + length]
            peak = jnp.max(s, axis=1, keepdims=True)
            p = jnp.exp(s - peak)
            total = jnp.sum(p, axis=1, keepdims=True)
            o = dot(p.astype(jnp.bfloat16), vt, 1, 1) / total
            mixed_ref[h * head_size : (h + 1) * head_size, i * rows : (i + 1) * rows] = o.T.astype(jnp.bfloat16)


def in_vmem(count):
    return [pl.BlockSpec(memory_space=pltpu.VMEM)] * count


def attention_forward(inputs, gain, wq, wk, wv, bias_values, heads, head_size, rows=256):
    length = inputs.shape[0]
    hd = heads * head_size
    return pl.pallas_call(
        functools.partial(attention_forward_kernel, heads, head_size, rows),
        out_shape=(
            jax.ShapeDtypeStruct((hd, length), jnp.bfloat16),
            jax.ShapeDtypeStruct((3 * hd, length), jnp.bfloat16),
            jax.ShapeDtypeStruct(inputs.shape, jnp.bfloat16),
        ),
        in_specs=in_vmem(6),
        out_specs=tuple(in_vmem(3)),
        scratch_shapes=[pltpu.VMEM((rows, bias_values.shape[1]), jnp.float32)],
        compiler_params=pltpu.CompilerParams(vmem_limit_bytes=VMEM_LIMIT),
        cost_estimate=cost("attention_forward"),
        name="attention_forward",
    )(inputs, gain, wq, wk, wv, bias_values)


def call(body, out_shape, args, name, flops, scratch=(), transcendentals=0):
    return pl.pallas_call(
        body,
        out_shape=out_shape,
        in_specs=in_vmem(len(args)),
        out_specs=jax.tree.map(lambda _: in_vmem(1)[0], out_shape),
        scratch_shapes=list(scratch),
        compiler_params=pltpu.CompilerParams(vmem_limit_bytes=VMEM_LIMIT),
        cost_estimate=cost(name),
        name=name,
    )(*args)


def shape(dims, dtype=jnp.bfloat16):
    return jax.ShapeDtypeStruct(dims, dtype)


def join(refs, target):
    at = 0
    for ref in refs:
        target[at : at + ref.shape[0], :] = ref[...]
        at += ref.shape[0]


def route_tokens(mixed_pieces, ow_pieces, source, grad, pack, gain, router, sizes):
    shards = len(mixed_pieces)
    tokens, width = source.shape

    def body(*refs):
        mixed_refs, ow_refs = refs[:shards], refs[shards : 2 * shards]
        source_ref, grad_ref, pack_ref, gain_ref, router_ref = refs[2 * shards : 2 * shards + 5]
        middle_ref, routed_ref, probability_ref = refs[2 * shards + 5 : 2 * shards + 8]
        middle = source_ref[...]
        for m, o in zip(mixed_refs, ow_refs):
            middle = middle + dot(m[...], o[...])
        middle_ref[...] = middle
        spread = lax.rsqrt(jnp.mean(middle * middle, axis=1, keepdims=True) + 1e-06)
        routed = (middle * spread * gain_ref[...]).astype(jnp.bfloat16)
        routed_ref[...] = routed
        packed = dot(pack_ref[...], routed).astype(jnp.bfloat16)
        packed_grad = dot(pack_ref[...], grad_ref[...]).astype(jnp.bfloat16)
        at = 0
        for ref in refs[2 * shards + 8 :]:
            size = ref.shape[0] // 2
            ref[:size, :] = packed[at : at + size, :]
            ref[size:, :] = packed_grad[at : at + size, :]
            at += size
        logits = dot(routed, router_ref[...], 1, 1)
        powered = jnp.exp(logits - jnp.max(logits, axis=1, keepdims=True))
        probability_ref[...] = powered / jnp.sum(powered, axis=1, keepdims=True)

    out = (shape((tokens, width), jnp.float32), shape((tokens, width)), shape((tokens, router.shape[0]), jnp.float32))
    out = out + tuple(shape((2 * n, width)) for n in sizes)
    args = (*mixed_pieces, *ow_pieces, source, grad, pack, gain, router)
    return call(body, out, args, "route_tokens", 0)


def gated(rows, grads, router, mine):
    logits = dot(rows, router, 1, 1)
    powered = jnp.exp(logits - jnp.max(logits, axis=1, keepdims=True))
    gate = jnp.sum(powered * mine, axis=1, keepdims=True) / jnp.sum(powered, axis=1, keepdims=True)
    return (gate * grads.astype(jnp.float32)).astype(jnp.bfloat16)


def expert_units(rows, grads, in_parts, out, out_ref, grad_ref):
    at, before = 0, 0.0
    for part in in_parts:
        before = before + dot(rows[:, at : at + part.shape[0]], part)
        at += part.shape[0]
    value, slope = gelu_pair(before)
    out_ref[...] += dot(value.astype(jnp.bfloat16), out)
    before_grad = (dot(grads, out, 1, 1) * slope).astype(jnp.bfloat16)
    at = 0
    for part in in_parts:
        grad_ref[:, at : at + part.shape[0]] += dot(before_grad, part, 1, 1)
        at += part.shape[0]


def expert_near(pieces, router, mine, weights, part):
    count, width = part * len(pieces), pieces[0].shape[1]
    n = len(pieces)

    def body(*refs):
        router_ref, mine_ref, in0, out0, in1, out1, both_ref, out_ref, grad_ref = refs[n:]
        for i, ref in enumerate(refs[:n]):
            both_ref[i * part : (i + 1) * part, :] = ref[:part, :]
            both_ref[count + i * part : count + (i + 1) * part, :] = ref[part:, :]
        rows = both_ref[:count, :]
        both_ref[count:, :] = gated(rows, both_ref[count:, :], router_ref[...], mine_ref[...])
        out_ref[...] = jnp.zeros_like(out_ref)
        grad_ref[...] = jnp.zeros_like(grad_ref)
        for i, o in ((in0, out0), (in1, out1)):
            expert_units(rows, both_ref[count:, :], (i[...],), o[...], out_ref, grad_ref)

    out = (shape((2 * count, width)), shape((count, width), jnp.float32), shape((count, width), jnp.float32))
    return call(body, out, (*pieces, router, mine, *weights), "expert_near", 0)


def expert_far(both, out_before, grad_before, weights, part):
    count, width = out_before.shape

    def body(both_ref, out_ref, grad_ref, top0, rest0, top1, rest1, *refs):
        out_total, grad_total = refs[-2:]
        out_total[...] = out_ref[...]
        grad_total[...] = grad_ref[...]
        for top, rest in ((top0, rest0), (top1, rest1)):
            cut = width - top.shape[0]
            in_parts = (top[...], rest[:cut, :])
            expert_units(both_ref[:count, :], both_ref[count:, :], in_parts, rest[cut:, :], out_total, grad_total)
        for i, ref in enumerate(refs[:-2]):
            ref[:part, :] = out_total[i * part : (i + 1) * part, :].astype(jnp.bfloat16)
            ref[part:, :] = grad_total[i * part : (i + 1) * part, :].astype(jnp.bfloat16)

    out = tuple(shape((2 * part, width)) for _ in range(count // part))
    scratch = [pltpu.VMEM((count, width), jnp.float32)] * 2
    return list(call(body, out, (both, out_before, grad_before, *weights), "expert_far", 0, scratch))


def token_grads(back, pack_t, middle, routed, probability, chosen, grad, gain, router, ow_pieces):
    tokens, width = middle.shape
    n, shards = len(back), len(ow_pieces)
    hd = ow_pieces[0].shape[0]

    def body(*refs):
        pack_ref, middle_ref, routed_ref, probability_ref, chosen_ref, g_ref, gain_ref, router_ref = refs[n : n + 8]
        ow_refs = refs[n + 8 : n + 8 + shards]
        result_ref, grad_out_ref, router_part_ref, gain_part_ref = refs[n + 8 + shards : n + 12 + shards]
        mixed_refs = refs[n + 12 + shards : n + 12 + 2 * shards]
        buffer = refs[-1]
        g = g_ref[...].astype(jnp.float32)
        middle = middle_ref[...]
        chosen = chosen_ref[...]
        probability = probability_ref[...]
        gate = jnp.sum(probability * chosen, axis=1, keepdims=True)
        half = buffer.shape[0] // n
        for i, ref in enumerate(refs[:n]):
            buffer[i * half : (i + 1) * half, :] = ref[:half, :]
        rows = dot(pack_ref[...], buffer[...])
        result_ref[...] = (middle + gate * rows).astype(jnp.bfloat16)
        gate_grad = jnp.sum(g * rows, axis=1, keepdims=True)
        logit_grad = (gate_grad * gate * (chosen - probability)).astype(jnp.bfloat16)
        router_part_ref[...] = dot(logit_grad, routed_ref[...], 0, 0)
        for i, ref in enumerate(refs[:n]):
            buffer[i * half : (i + 1) * half, :] = ref[half:, :]
        routed_grad = dot(logit_grad, router_ref[...]) + dot(pack_ref[...], buffer[...])
        spread = lax.rsqrt(jnp.mean(middle * middle, axis=1, keepdims=True) + 1e-06)
        gain_part_ref[...] = jnp.sum(routed_grad * middle * spread, axis=0, keepdims=True)
        u = routed_grad * gain_ref[...]
        mean = jnp.mean(u * middle, axis=1, keepdims=True)
        middle_grad = (g + spread * u - middle * (spread * spread * spread * mean)).astype(jnp.bfloat16)
        grad_out_ref[...] = middle_grad
        for m, o in zip(mixed_refs, ow_refs):
            m[...] = dot(middle_grad, o[...], 1, 1).astype(jnp.bfloat16)

    out = (
        shape((tokens, width)),
        shape((tokens, width)),
        shape(router.shape, jnp.float32),
        shape((1, width), jnp.float32),
    ) + (shape((tokens, hd)),) * shards
    args = (*back, pack_t, middle, routed, probability, chosen, grad, gain, router, *ow_pieces)
    scratch = [pltpu.VMEM((pack_t.shape[1], width), jnp.bfloat16)]
    return call(body, out, args, "token_grads", 0, scratch)


def cut_halves(part, bit, keep_ref, sent_ref):
    half = keep_ref.shape[0]
    keep_ref[...] = part[pl.ds(pl.multiple_of(bit * half, half), half), :]
    sent_ref[...] = part[pl.ds(pl.multiple_of((1 - bit) * half, half), half), :].astype(jnp.bfloat16)


def weight_part(head_ref, normed_ref, weight_refs, h, part, at):
    value = dot(head_ref[...], normed_ref[...])
    part[at : at + value.shape[0], :] = value
    size = value.shape[0] // 3
    gain = jnp.zeros((1, value.shape[1]), jnp.float32)
    for c, ref in enumerate(weight_refs):
        weight = ref[h * size : (h + 1) * size, :].astype(jnp.float32)
        gain = gain + jnp.sum(weight * value[c * size : (c + 1) * size, :], axis=0, keepdims=True)
    return gain


def place_grads(pieces, perm):
    tokens, hd = pieces[0].shape
    n = len(pieces)

    def body(*refs):
        perm_ref, out_ref = refs[n : n + 2]
        buffer = refs[-1]
        join(refs[:n], buffer)
        out_ref[...] = dot(buffer[...], perm_ref[...], 0, 0).astype(jnp.bfloat16)

    scratch = [pltpu.VMEM((n * tokens, hd), jnp.bfloat16)]
    return call(body, shape((hd, perm.shape[1])), (*pieces, perm), "place_grads", 0, scratch)


def first_parts(normed, head_grads, weights, middle_pieces, back, mixed_t, high):
    width = normed.shape[1]
    rows = head_grads[0].shape[0]
    n, hd = len(head_grads), mixed_t.shape[0]
    total = rows * n + hd

    def body(high_ref, normed_ref, wq_ref, wk_ref, wv_ref, back_ref, mixed_ref, *refs):
        keep_ref, sent_ref, gain_ref, middle_ref, part, buffer = refs[n + len(middle_pieces) :]
        gain = jnp.zeros(gain_ref.shape, jnp.float32)
        for h, ref in enumerate(refs[:n]):
            gain = gain + weight_part(ref, normed_ref, (wq_ref, wk_ref, wv_ref), h, part, h * rows)
        gain_ref[...] = gain
        join(refs[n : n + len(middle_pieces)], buffer)
        middle_ref[...] = dot(back_ref[...], buffer[...]).astype(jnp.bfloat16)
        part[n * rows :, :] = dot(mixed_ref[...], middle_ref[...])
        cut_halves(part, high_ref[0], keep_ref, sent_ref)

    out = (
        shape((total // 2, width), jnp.float32),
        shape((total // 2, width)),
        shape((1, width), jnp.float32),
        shape(normed.shape),
    )
    args = (normed, *weights, back, mixed_t, *head_grads, *middle_pieces)
    scratch = [pltpu.VMEM((total, width), jnp.float32), pltpu.VMEM((back.shape[1], width), jnp.bfloat16)]
    return with_bit(body, out, args, high, "first_parts", scratch)


def with_bit(body, out, args, high, name, scratch=()):
    return pl.pallas_call(
        body,
        out_shape=out,
        in_specs=[pl.BlockSpec(memory_space=pltpu.SMEM)] + in_vmem(len(args)),
        out_specs=jax.tree.map(lambda _: in_vmem(1)[0], out),
        scratch_shapes=list(scratch),
        compiler_params=pltpu.CompilerParams(vmem_limit_bytes=VMEM_LIMIT),
        cost_estimate=cost(name),
        name=name,
    )(high, *args)


def last_parts(normed, head_grad, weights, h, gain_before, gain, small, high):
    width = normed.shape[1]
    rows = head_grad.shape[0]
    total = rows + small.shape[0]

    def body(high_ref, normed_ref, head_ref, wq_ref, wk_ref, wv_ref, before_ref, gain_ref, small_ref, *refs):
        keep_ref, sent_ref, part = refs
        gain_part = weight_part(head_ref, normed_ref, (wq_ref, wk_ref, wv_ref), h, part, 0)
        line = lax.broadcasted_iota(jnp.int32, small_ref.shape, 0)
        gain_part = (before_ref[...] + gain_part) / gain_ref[...]
        part[rows:, :] = jnp.where(line == 0, gain_part, small_ref[...])
        cut_halves(part, high_ref[0], keep_ref, sent_ref)

    out = (shape((total // 2, width), jnp.float32), shape((total // 2, width)))
    args = (normed, head_grad, *weights, gain_before, gain, small)
    return with_bit(body, out, args, high, "last_parts", [pltpu.VMEM((total, width), jnp.float32)])


def place_sums(first, last, bits, heads, head_size):
    width = first[0].shape[1]
    hd = heads * head_size
    totals = (2 * first[0].shape[0], 2 * last[0].shape[0])

    def body(bits_ref, a0, a1, b0, b1, q_ref, k_ref, v_ref, o_ref, first_sum, last_sum):
        for i, (own, other, target) in enumerate(((a0, a1, first_sum), (b0, b1, last_sum))):
            half = own.shape[0]
            target[pl.ds(pl.multiple_of(bits_ref[i] * half, half), half), :] = own[...].astype(jnp.float32)
            target[pl.ds(pl.multiple_of((1 - bits_ref[i]) * half, half), half), :] = other[...].astype(jnp.float32)
        for h in range(heads):
            source, at = (first_sum, 3 * h * head_size) if h < heads - 1 else (last_sum, 0)
            for c, ref in enumerate((q_ref, k_ref, v_ref)):
                start = at + c * head_size
                ref[h * head_size : (h + 1) * head_size, :] = source[start : start + head_size, :]
        o_ref[...] = first_sum[3 * (heads - 1) * head_size :, :]

    out = (shape((hd, width), jnp.float32),) * 4
    scratch = [pltpu.VMEM((total, width), jnp.float32) for total in totals]
    return with_bit(body, out, (*first, *last), bits, "place_sums", scratch)


def place_halves(own, other, low):
    half, width = own.shape

    def body(low_ref, own_ref, other_ref, out_ref):
        out_ref[pl.ds(pl.multiple_of(low_ref[0] * half, half), half), :] = own_ref[...]
        out_ref[pl.ds(pl.multiple_of((1 - low_ref[0]) * half, half), half), :] = other_ref[...]

    return with_bit(body, shape((2 * half, width), own.dtype), (own, other), low.reshape(1), "place_halves")


def expert_weights(both_all, w_in, w_out):
    shards, _, count, width = both_all.shape

    def body(both_ref, wi_ref, wo_ref, in_ref, out_ref):
        for s in range(shards):
            rows, grads = both_ref[s, 0], both_ref[s, 1]
            value, slope = gelu_pair(dot(rows, wi_ref[...]))
            before_grad = (dot(grads, wo_ref[...], 1, 1) * slope).astype(jnp.bfloat16)
            part_in = dot(rows, before_grad, 0, 0)
            part_out = dot(value.astype(jnp.bfloat16), grads, 0, 0)
            if s == 0:
                in_ref[...] = part_in
                out_ref[...] = part_out
            else:
                in_ref[...] += part_in
                out_ref[...] += part_out

    out = (shape(w_in.shape, jnp.float32), shape(w_out.shape, jnp.float32))
    return call(body, out, (both_all, w_in, w_out), "expert_weights", 10**10)


def attention_backward_kernel(h, heads, head_size, rows, qkv_ref, bias_ref, grad_ref, out_ref, diag_ref, strip_ref, total_ref):
    length = qkv_ref.shape[1]
    blocks = length // rows
    hd = heads * head_size
    width = bias_ref.shape[1]
    strip_ref[...] = bias_strip(bias_ref[h : h + 1, :], rows)
    total_ref[...] = jnp.zeros_like(total_ref)
    qt32 = qkv_ref[h * head_size : (h + 1) * head_size, :].astype(jnp.float32) * 0.125
    qt = qt32.astype(jnp.bfloat16)
    q = qt32.T.astype(jnp.bfloat16)
    kt = qkv_ref[hd + h * head_size : hd + (h + 1) * head_size, :]
    k = kt.astype(jnp.float32).T.astype(jnp.bfloat16)
    vt = qkv_ref[2 * hd + h * head_size : 2 * hd + (h + 1) * head_size, :]
    gt = grad_ref[h * head_size : (h + 1) * head_size, :]
    g = gt.astype(jnp.float32).T.astype(jnp.bfloat16)
    dk = jnp.zeros((head_size, length), jnp.float32)
    dv = jnp.zeros((head_size, length), jnp.float32)
    for i in range(blocks):
        at = (blocks - 1 - i) * rows
        part = slice(i * rows, (i + 1) * rows)
        s = dot(q[part], kt) + strip_ref[:, at : at + length]
        peak = jnp.max(s, axis=1, keepdims=True)
        p = jnp.exp(s - peak)
        p = p * (1.0 / jnp.sum(p, axis=1, keepdims=True))
        dp = dot(g[part], vt)
        delta = jnp.sum(p * dp, axis=1, keepdims=True)
        ds = p * (dp - delta)
        total_ref[:, at : at + length] += ds
        dsb = ds.astype(jnp.bfloat16)
        dv = dv + dot(gt[:, part], p.astype(jnp.bfloat16))
        dk = dk + dot(qt[:, part], dsb)
        dq = dot(dsb, k) * 0.125
        out_ref[0:head_size, part] = dq.T.astype(jnp.bfloat16)
    out_ref[head_size : 2 * head_size, :] = dk.astype(jnp.bfloat16)
    out_ref[2 * head_size : 3 * head_size, :] = dv.astype(jnp.bfloat16)
    folded = total_ref[...]
    half = rows // 2
    while half:
        folded = folded[:half] + pltpu.roll(folded[half:], width - half, 1)
        half //= 2
    diag_ref[...] = pltpu.roll(folded, rows - 1, 1)


def attention_backward(qkv_t, bias_values, grad_t, h, heads, head_size, rows=256):
    length = qkv_t.shape[1]
    width = bias_values.shape[1]
    return pl.pallas_call(
        functools.partial(attention_backward_kernel, h, heads, head_size, rows),
        out_shape=(jax.ShapeDtypeStruct((3 * head_size, length), jnp.bfloat16), jax.ShapeDtypeStruct((1, width), jnp.float32)),
        in_specs=[pl.BlockSpec(memory_space=pltpu.VMEM)] * 3,
        out_specs=(pl.BlockSpec(memory_space=pltpu.VMEM),) * 2,
        scratch_shapes=[pltpu.VMEM((rows, width), jnp.float32)] * 2,
        compiler_params=pltpu.CompilerParams(vmem_limit_bytes=VMEM_LIMIT),
        cost_estimate=cost("attention_backward"),
        name="attention_backward",
    )(qkv_t, bias_values, grad_t)


def gelu_pair(v):
    inner = 0.7978845608028654 * (v + 0.044715 * v * v * v)
    t = jnp.tanh(inner)
    slope = 0.7978845608028654 * (1.0 + 3.0 * 0.044715 * v * v)
    return 0.5 * v * (1.0 + t), 0.5 * (1.0 + t) + 0.5 * v * (1.0 - t * t) * slope


def swap(x, axis, k):
    return lax.ppermute(x, axis, [(i, i ^ k) for i in range(lax.axis_size(axis))])


def gather_relative(x, axis="shard"):
    pieces = {0: x}
    bit = lax.axis_size(axis) // 2
    while bit:
        for k in sorted(pieces):
            pieces[k ^ bit] = swap(pieces[k], axis, bit)
        bit //= 2
    return [pieces[k] for k in range(len(pieces))]


def exchange_relative(pieces, axis):
    return [p if k == 0 else swap(p, axis, k) for k, p in enumerate(pieces)]


def exchange_window(pieces, axis, window):
    received = [pieces[0]]
    for k in range(1, len(pieces)):
        sent = pieces[k]
        if k > window:
            sent, received[k - window] = lax.optimization_barrier((sent, received[k - window]))
        received.append(swap(sent, axis, k))
    return received


def sum_pairs(x, axis):
    if lax.axis_size(axis) != 4:
        return lax.psum(x, axis)
    one, two, three = (swap(x, axis, k) for k in (1, 2, 3))
    return (x + one) + (two + three)


def sum_all(x, axis):
    if lax.axis_size(axis) > 8:
        return lax.psum(x, axis)
    bit = 1
    while bit < lax.axis_size(axis):
        x = x + swap(x, axis, bit)
        bit *= 2
    return x


def bit_of(me, bit):
    return (me & bit) // bit


def halving(keep, sent, axis, bits):
    me = lax.axis_index(axis)
    for i, bit in enumerate(bits):
        x = keep + (yield swap(sent, axis, bit)).astype(jnp.float32)
        if i + 1 < len(bits):
            half = x.shape[0] // 2
            high = bit_of(me, bits[i + 1])
            sent = lax.dynamic_slice_in_dim(x, (1 - high) * half, half, 0).astype(jnp.bfloat16)
            keep = lax.dynamic_slice_in_dim(x, high * half, half, 0)
    x = lax.optimization_barrier(x.astype(jnp.bfloat16))
    for bit in reversed(bits):
        other = yield swap(x, axis, bit)
        if bit != bits[0]:
            high = bit_of(me, bit)
            x = jnp.concatenate([jnp.where(high == 0, x, other), jnp.where(high == 0, other, x)], axis=0)
    yield x, other


def together(*arrays):
    return lax.optimization_barrier(arrays)


def on_device(
    inputs,
    cotangent,
    expert_id,
    slot_index,
    bucket_ids,
    attention_gain,
    query_weight,
    key_weight,
    value_weight,
    output_weight,
    bias_table,
    expert_gain,
    router_weight,
    expert_in,
    expert_out,
):
    bf16, f32 = jnp.bfloat16, jnp.float32
    length, width = inputs.shape
    buckets, heads = bias_table.shape
    hd = query_weight.shape[1]
    head_size = hd // heads
    experts = router_weight.shape[1]
    expert_devices = lax.axis_size("expert")
    shards = lax.axis_size("shard")
    me_e = lax.axis_index("expert")
    me_s = lax.axis_index("shard")
    part = max(1, 3 * length // (2 * experts * shards))
    owned = -(-(length + experts * (shards - 1)) // (16 * shards)) * 16
    relative = expert_devices <= 8
    w_in, w_out = expert_in[0], expert_out[0]

    sizes = [part] * expert_devices

    def exchange_experts(pieces):
        if relative:
            return exchange_window(pieces, "expert", 4)
        blocks = jnp.stack(pieces)
        return list(lax.all_to_all(blocks, "expert", 0, 0))

    ow_pieces = gather_relative(output_weight)
    cut = 2 * w_in.shape[0] // 3
    far_top = swap(w_in[:cut], "shard", 2)

    w_rows = (query_weight.T, key_weight.T, value_weight.T)
    router_rows = router_weight.T

    residue = slot_index % shards
    group = slot_index // shards
    order = jnp.arange(length, dtype=jnp.int32)
    earlier = (order[None, :] < order[:, None]) & (residue[None, :] == residue[:, None])
    rank = jnp.sum(earlier.astype(jnp.int32), axis=1)
    place = (residue ^ me_s) * owned + rank
    numbers = jnp.arange(shards * owned, dtype=jnp.int32)[:, None]
    perm_flag = numbers == place[None, :]
    perm = lax.optimization_barrier(perm_flag.astype(bf16))
    own_flag = perm_flag[:owned]
    own = perm[:owned]

    def packing(expert):
        target = jnp.where(group < part, expert * part + group, -1)
        target_own = jnp.sum(jnp.where(own_flag, target[None, :] + 1, 0), axis=1) - 1
        numbers_own = jnp.arange(experts * part, dtype=jnp.int32)
        return (
            (numbers_own[:, None] == target_own[None, :]).astype(bf16),
            (numbers_own[None, :] == target_own[:, None]).astype(bf16),
        )

    pack, pack_t = packing(expert_id ^ me_e if relative else expert_id)
    expert_own = jnp.sum(jnp.where(own_flag, expert_id[None, :], 0), axis=1)

    offsets = jnp.concatenate([bucket_ids[1:, 0][::-1], bucket_ids[0, :], jnp.full((1,), -1, jnp.int32)])
    bucket_flag = offsets[None, :] == jnp.arange(buckets, dtype=jnp.int32)[:, None]
    bias_values = jnp.sum(jnp.where(bucket_flag[None], bias_table.T[:, :, None], 0.0), axis=1)
    mixed_t, qkv_t, normed = attention_forward(
        inputs, attention_gain[None, :], *w_rows, bias_values, heads, head_size
    )
    mixed_t, *ow_pieces = lax.optimization_barrier((mixed_t, *ow_pieces))
    mixed = dot(perm, mixed_t, 1, 1).astype(bf16)
    place, rank, mixed = lax.optimization_barrier((place, rank, mixed))
    back = lax.optimization_barrier((place[:, None] == numbers.T).astype(bf16))
    back_absolute = lax.optimization_barrier(((residue * owned + rank)[:, None] == numbers.T).astype(bf16))
    mixed_own = exchange_relative([mixed[k * owned : (k + 1) * owned] for k in range(shards)], "shard")
    _, rest_in, rest_out = together(mixed[:1], w_in[cut:], w_out)
    rest = jnp.concatenate([rest_in, rest_out], axis=0)
    source_own = dot(own, inputs)
    grad_own = dot(own, cotangent).astype(bf16)

    far_top, near_in, near_out, rest, *mixed_own = lax.optimization_barrier((far_top, w_in, w_out, rest, *mixed_own))
    far_rest = swap(rest, "shard", 2)
    near_in, near_out, last_top = swap(near_in, "shard", 1), swap(near_out, "shard", 1), swap(far_top, "shard", 1)

    middle, routed, probability, *pieces = route_tokens(
        mixed_own, ow_pieces, source_own, grad_own, pack, expert_gain[None, :], router_rows, sizes
    )
    near_in, near_out, last_top, *pieces = lax.optimization_barrier((near_in, near_out, last_top, *pieces))
    pieces = exchange_experts(pieces)
    far_rest, *pieces = lax.optimization_barrier((far_rest, *pieces))
    last_rest = swap(far_rest, "shard", 1)

    mine = (jnp.arange(experts, dtype=jnp.int32)[None, :] == me_e).astype(f32)
    both, out_near, grad_near = expert_near(pieces, router_rows, mine, (w_in, w_out, near_in, near_out), part)
    both_all = lax.all_gather(both.reshape(2, expert_devices * part, width), "shard", axis=0)
    out_near, last_rest = lax.optimization_barrier((out_near, last_rest))
    far_all = (far_top, far_rest, last_top, last_rest)
    back_pieces = exchange_experts(expert_far(both, out_near, grad_near, far_all, part))
    in_gradient, out_gradient = expert_weights(both_all, w_in, w_out)
    in_gradient, out_gradient, *back_pieces = together(in_gradient, out_gradient, *back_pieces)

    chosen = (expert_own[:, None] == jnp.arange(experts, dtype=jnp.int32)[None, :]).astype(f32)
    result_own, attention_grad, router_part, expert_gain_part, *mixed_grad = token_grads(
        back_pieces, pack_t, middle, routed, probability, chosen, grad_own, expert_gain[None, :],
        router_rows, ow_pieces,
    )
    mixed_grad = exchange_relative(mixed_grad, "shard")
    attention_grad, *mixed_grad = lax.optimization_barrier((attention_grad, *mixed_grad))
    far_grad, near_grad = swap(attention_grad, "shard", 2), swap(attention_grad, "shard", 1)
    mixed_grad_t = place_grads(mixed_grad, perm)

    w_heads = jnp.concatenate([w[h * head_size : (h + 1) * head_size] for h in range(heads) for w in w_rows], axis=0)
    bits = [1 << i for i in range(expert_devices.bit_length() - 1)]
    bits_first, bits_last = bits, [*bits[1:2], *bits[:1], *bits[2:]]
    high_first, high_last = bit_of(me_e, bits_first[0]).reshape(1), bit_of(me_e, bits_last[0]).reshape(1)
    head_grads, diagonals = [], []
    for h in range(heads):
        if h == heads - 1:
            keep_first, sent_first, gain_first, middle_grad_all = first_parts(
                normed, head_grads, w_rows, attention_grads, back, mixed_t, high_first
            )
            mixed_grad_t, sent_first, middle_grad_all = lax.optimization_barrier(
                (mixed_grad_t, sent_first, middle_grad_all)
            )
        head_grad, diagonal = attention_backward(qkv_t, bias_values, mixed_grad_t, h, heads, head_size)
        if h == 0:
            far_grad, near_grad, head_grad, result_own = together(far_grad, near_grad, head_grad, result_own)
            results = lax.all_gather(result_own, "shard", axis=0, tiled=True)
            attention_grads = [attention_grad, near_grad, far_grad, swap(far_grad, "shard", 1)]
        if h == heads - 1 and relative:
            sums_first = halving(keep_first, sent_first, "expert", bits_first)
            first, head_grad, diagonal = together(next(sums_first), head_grad, diagonal)
        head_grads.append(head_grad)
        diagonals.append(diagonal)
    qkv_grad_t = jnp.concatenate(head_grads, axis=0)

    normed_part = dot(qkv_grad_t, w_heads, 0, 0)
    half = length // 2
    low = me_s % 2
    other_half = lax.dynamic_slice_in_dim(normed_part, (1 - low) * half, half, 0)
    own_half = lax.dynamic_slice_in_dim(normed_part, low * half, half, 0)
    near_part = swap(other_half.astype(bf16), "shard", 1)
    if relative:
        first = sums_first.send(first)

    table_part = jnp.sum(jnp.where(bucket_flag[None], jnp.stack(diagonals), 0.0), axis=2).reshape(1, -1)
    table_part = jnp.pad(table_part, ((0, 0), (0, width - table_part.shape[1])))
    small = jnp.concatenate([jnp.zeros_like(table_part), expert_gain_part, router_part, table_part], axis=0)
    small = jnp.pad(small, ((0, -small.shape[0] % 64), (0, 0)))
    keep_last, sent_last = last_parts(
        normed, head_grads[-1], w_rows, heads - 1, gain_first, attention_gain[None, :], small, high_last
    )
    if relative:
        first, near_part, keep_last, results = together(first, near_part, keep_last, results)
        result = dot(back_absolute, results).astype(bf16)
        near_sum = lax.optimization_barrier((own_half + near_part.astype(f32)).astype(bf16))
        far_sum = swap(near_sum, "shard", 2)
        sums_last = halving(keep_last, sent_last, "expert", bits_last)
        first, last = together(sums_first.send(first), next(sums_last))
        for step in range(2 * len(bits) - 3):
            first, last = sums_first.send(first), sums_last.send(last)
            if step == 0:
                far_sum, first, last = together(far_sum, first, last)
            elif step == 1:
                result, first, last = together(result, first, last)
            else:
                first, last = together(first, last)
        first = sums_first.send(first)
        for _ in range(2):
            last = sums_last.send(last)
        last = sums_last.send(last)
    else:
        whole = []
        for keep, sent, high in ((keep_first, sent_first, high_first), (keep_last, sent_last, high_last)):
            sent = sent.astype(f32)
            low_part, high_part = jnp.where(high == 0, keep, sent), jnp.where(high == 0, sent, keep)
            low_part, high_part = lax.psum((low_part, high_part), "expert")
            whole.append((jnp.where(high == 0, low_part, high_part), jnp.where(high == 0, high_part, low_part)))
        first, last = whole
        near_sum = lax.optimization_barrier((own_half + near_part.astype(f32)).astype(bf16))
        far_sum = swap(near_sum, "shard", 2)
    if not relative:
        result = dot(back_absolute, results).astype(bf16)
    normed_grad = near_sum.astype(f32) + far_sum.astype(f32)
    source_half = lax.dynamic_slice_in_dim(inputs, low * half, half, 0).astype(f32)
    inverse_half = lax.rsqrt(jnp.mean(source_half * source_half, axis=-1, keepdims=True) + 1e-06)
    middle_half = lax.dynamic_slice_in_dim(middle_grad_all, low * half, half, 0).astype(f32)
    w = normed_grad * attention_gain
    grad_half = middle_half + inverse_half * w - source_half * (
        inverse_half * inverse_half * inverse_half * jnp.mean(w * source_half, axis=-1, keepdims=True)
    )
    grad_other = swap(grad_half, "shard", 1)
    input_gradient = place_halves(grad_half, grad_other, low)
    input_gradient, *last = together(input_gradient, *last)
    query_gradient, key_gradient, value_gradient, output_gradient = place_sums(
        first, last, jnp.concatenate([high_first, high_last]), heads, head_size
    )
    small = jnp.where(high_last == 0, last[1], last[0])[last[0].shape[0] - small.shape[0] :].astype(f32)
    table_gradient = small[2 + experts, : buckets * heads].reshape(heads, buckets).T
    small = sum_pairs(small[: 2 + experts], "shard")

    return (
        result,
        input_gradient,
        small[0],
        query_gradient.T,
        key_gradient.T,
        value_gradient.T,
        output_gradient,
        table_gradient,
        small[1],
        small[2:].T,
        in_gradient[None],
        out_gradient[None],
    )


def solution(mesh):
    placed = (
        P("expert", None),
        P("expert", None),
        P("expert"),
        P("expert"),
        P(),
        P(),
        P(None, "shard"),
        P(None, "shard"),
        P(None, "shard"),
        P("shard", None),
        P(None, "shard"),
        P(),
        P(),
        P("expert", None, "shard"),
        P("expert", "shard", None),
    )
    return jax.shard_map(
        on_device,
        mesh=mesh,
        in_specs=placed,
        out_specs=(
            P("expert", None),
            P("expert", None),
            P(),
            P(None, "shard"),
            P(None, "shard"),
            P(None, "shard"),
            P("shard", None),
            P(None, "shard"),
            P(),
            P(),
            P("expert", None, "shard"),
            P("expert", "shard", None),
        ),
        check_vma=False,
    )
```

```python
import functools
import jax
import jax.numpy as jnp
from jax import lax
from jax.experimental import pallas as pl
from jax.experimental.pallas import tpu as pltpu
from jax.sharding import PartitionSpec as P

TIMES = {"attention_forward": 9.4, "attention_backward": 6.7, "route_tokens": 4.7, "expert_near": 8.4, "expert_far": 9.6, "token_grads": 5.0, "first_parts": 8.0, "last_parts": 3.2, "place_sums": 2.9, "place_halves": 3.8, "expert_weights": 14.3, "place_grads": 3.4}


def cost(name):
    return pl.CostEstimate(flops=int(TIMES[name] * 1.15e9), bytes_accessed=10**5, transcendentals=0)


VMEM_LIMIT = 56 * 1024 * 1024


def dot(a, b, ca=1, cb=0):
    return lax.dot_general(a, b, (((ca,), (cb,)), ((), ())), preferred_element_type=jnp.float32)


def bias_strip(values_row, rows):
    total = values_row.shape[-1]
    wide = jnp.broadcast_to(values_row.reshape(1, total), (rows, total))
    return pltpu.roll(wide, total - rows + 1, 1, stride=1, stride_axis=0)


def attention_forward_kernel(heads, head_size, rows, in_ref, gain_ref, wq_ref, wk_ref, wv_ref, bias_ref, mixed_ref, qkv_ref, normed_ref, strip_ref):
    length = in_ref.shape[0]
    blocks = length // rows
    hd = heads * head_size
    source = in_ref[...].astype(jnp.float32)
    inverse = lax.rsqrt(jnp.mean(source * source, axis=1, keepdims=True) + 1e-06)
    normed_ref[...] = (source * inverse * gain_ref[...]).astype(jnp.bfloat16)
    for at, ref in enumerate((wq_ref, wk_ref, wv_ref)):
        qkv_ref[at * hd : (at + 1) * hd, :] = dot(ref[...], normed_ref[...], 1, 1).astype(jnp.bfloat16)
    for h in range(heads):
        strip_ref[...] = bias_strip(bias_ref[h : h + 1, :], rows)
        q = (qkv_ref[h * head_size : (h + 1) * head_size, :].astype(jnp.float32) * 0.125).T.astype(jnp.bfloat16)
        kt = qkv_ref[hd + h * head_size : hd + (h + 1) * head_size, :]
        vt = qkv_ref[2 * hd + h * head_size : 2 * hd + (h + 1) * head_size, :]
        for i in range(blocks):
            s = dot(q[i * rows : (i + 1) * rows], kt)
            at = (blocks - 1 - i) * rows
            s = s + strip_ref[:, at : at + length]
            peak = jnp.max(s, axis=1, keepdims=True)
            p = jnp.exp(s - peak)
            total = jnp.sum(p, axis=1, keepdims=True)
            o = dot(p.astype(jnp.bfloat16), vt, 1, 1) / total
            mixed_ref[h * head_size : (h + 1) * head_size, i * rows : (i + 1) * rows] = o.T.astype(jnp.bfloat16)


def in_vmem(count):
    return [pl.BlockSpec(memory_space=pltpu.VMEM)] * count


def attention_forward(inputs, gain, wq, wk, wv, bias_values, heads, head_size, rows=256):
    length = inputs.shape[0]
    hd = heads * head_size
    return pl.pallas_call(
        functools.partial(attention_forward_kernel, heads, head_size, rows),
        out_shape=(
            jax.ShapeDtypeStruct((hd, length), jnp.bfloat16),
            jax.ShapeDtypeStruct((3 * hd, length), jnp.bfloat16),
            jax.ShapeDtypeStruct(inputs.shape, jnp.bfloat16),
        ),
        in_specs=in_vmem(6),
        out_specs=tuple(in_vmem(3)),
        scratch_shapes=[pltpu.VMEM((rows, bias_values.shape[1]), jnp.float32)],
        compiler_params=pltpu.CompilerParams(vmem_limit_bytes=VMEM_LIMIT),
        cost_estimate=cost("attention_forward"),
        name="attention_forward",
    )(inputs, gain, wq, wk, wv, bias_values)


def call(body, out_shape, args, name, flops, scratch=(), transcendentals=0):
    return pl.pallas_call(
        body,
        out_shape=out_shape,
        in_specs=in_vmem(len(args)),
        out_specs=jax.tree.map(lambda _: in_vmem(1)[0], out_shape),
        scratch_shapes=list(scratch),
        compiler_params=pltpu.CompilerParams(vmem_limit_bytes=VMEM_LIMIT),
        cost_estimate=cost(name),
        name=name,
    )(*args)


def shape(dims, dtype=jnp.bfloat16):
    return jax.ShapeDtypeStruct(dims, dtype)


def join(refs, target):
    at = 0
    for ref in refs:
        target[at : at + ref.shape[0], :] = ref[...]
        at += ref.shape[0]


def route_tokens(mixed_pieces, ow_pieces, source, grad, pack, gain, router, sizes):
    shards = len(mixed_pieces)
    tokens, width = source.shape

    def body(*refs):
        mixed_refs, ow_refs = refs[:shards], refs[shards : 2 * shards]
        source_ref, grad_ref, pack_ref, gain_ref, router_ref = refs[2 * shards : 2 * shards + 5]
        middle_ref, routed_ref, probability_ref = refs[2 * shards + 5 : 2 * shards + 8]
        middle = source_ref[...]
        for m, o in zip(mixed_refs, ow_refs):
            middle = middle + dot(m[...], o[...])
        middle_ref[...] = middle
        spread = lax.rsqrt(jnp.mean(middle * middle, axis=1, keepdims=True) + 1e-06)
        routed = (middle * spread * gain_ref[...]).astype(jnp.bfloat16)
        routed_ref[...] = routed
        packed = dot(pack_ref[...], routed).astype(jnp.bfloat16)
        packed_grad = dot(pack_ref[...], grad_ref[...]).astype(jnp.bfloat16)
        at = 0
        for ref in refs[2 * shards + 8 :]:
            size = ref.shape[0] // 2
            ref[:size, :] = packed[at : at + size, :]
            ref[size:, :] = packed_grad[at : at + size, :]
            at += size
        logits = dot(routed, router_ref[...], 1, 1)
        powered = jnp.exp(logits - jnp.max(logits, axis=1, keepdims=True))
        probability_ref[...] = powered / jnp.sum(powered, axis=1, keepdims=True)

    out = (shape((tokens, width), jnp.float32), shape((tokens, width)), shape((tokens, router.shape[0]), jnp.float32))
    out = out + tuple(shape((2 * n, width)) for n in sizes)
    args = (*mixed_pieces, *ow_pieces, source, grad, pack, gain, router)
    return call(body, out, args, "route_tokens", 0)


def gated(rows, grads, router, mine):
    logits = dot(rows, router, 1, 1)
    powered = jnp.exp(logits - jnp.max(logits, axis=1, keepdims=True))
    gate = jnp.sum(powered * mine, axis=1, keepdims=True) / jnp.sum(powered, axis=1, keepdims=True)
    return (gate * grads.astype(jnp.float32)).astype(jnp.bfloat16)


def expert_units(rows, grads, in_parts, out, out_ref, grad_ref):
    at, before = 0, 0.0
    for part in in_parts:
        before = before + dot(rows[:, at : at + part.shape[0]], part)
        at += part.shape[0]
    value, slope = gelu_pair(before)
    out_ref[...] += dot(value.astype(jnp.bfloat16), out)
    before_grad = (dot(grads, out, 1, 1) * slope).astype(jnp.bfloat16)
    at = 0
    for part in in_parts:
        grad_ref[:, at : at + part.shape[0]] += dot(before_grad, part, 1, 1)
        at += part.shape[0]


def expert_near(pieces, router, mine, weights, part):
    count, width = part * len(pieces), pieces[0].shape[1]
    n = len(pieces)

    def body(*refs):
        router_ref, mine_ref, in0, out0, in1, out1, both_ref, out_ref, grad_ref = refs[n:]
        for i, ref in enumerate(refs[:n]):
            both_ref[i * part : (i + 1) * part, :] = ref[:part, :]
            both_ref[count + i * part : count + (i + 1) * part, :] = ref[part:, :]
        rows = both_ref[:count, :]
        both_ref[count:, :] = gated(rows, both_ref[count:, :], router_ref[...], mine_ref[...])
        out_ref[...] = jnp.zeros_like(out_ref)
        grad_ref[...] = jnp.zeros_like(grad_ref)
        for i, o in ((in0, out0), (in1, out1)):
            expert_units(rows, both_ref[count:, :], (i[...],), o[...], out_ref, grad_ref)

    out = (shape((2 * count, width)), shape((count, width), jnp.float32), shape((count, width), jnp.float32))
    return call(body, out, (*pieces, router, mine, *weights), "expert_near", 0)


def expert_far(both, out_before, grad_before, weights, part):
    count, width = out_before.shape

    def body(both_ref, out_ref, grad_ref, top0, rest0, top1, rest1, *refs):
        out_total, grad_total = refs[-2:]
        out_total[...] = out_ref[...]
        grad_total[...] = grad_ref[...]
        for top, rest in ((top0, rest0), (top1, rest1)):
            cut = width - top.shape[0]
            in_parts = (top[...], rest[:cut, :])
            expert_units(both_ref[:count, :], both_ref[count:, :], in_parts, rest[cut:, :], out_total, grad_total)
        for i, ref in enumerate(refs[:-2]):
            ref[:part, :] = out_total[i * part : (i + 1) * part, :].astype(jnp.bfloat16)
            ref[part:, :] = grad_total[i * part : (i + 1) * part, :].astype(jnp.bfloat16)

    out = tuple(shape((2 * part, width)) for _ in range(count // part))
    scratch = [pltpu.VMEM((count, width), jnp.float32)] * 2
    return list(call(body, out, (both, out_before, grad_before, *weights), "expert_far", 0, scratch))


def token_grads(back, pack_t, middle, routed, probability, chosen, grad, gain, router, ow_pieces):
    tokens, width = middle.shape
    n, shards = len(back), len(ow_pieces)
    hd = ow_pieces[0].shape[0]

    def body(*refs):
        pack_ref, middle_ref, routed_ref, probability_ref, chosen_ref, g_ref, gain_ref, router_ref = refs[n : n + 8]
        ow_refs = refs[n + 8 : n + 8 + shards]
        result_ref, grad_out_ref, router_part_ref, gain_part_ref = refs[n + 8 + shards : n + 12 + shards]
        mixed_refs = refs[n + 12 + shards : n + 12 + 2 * shards]
        buffer = refs[-1]
        g = g_ref[...].astype(jnp.float32)
        middle = middle_ref[...]
        chosen = chosen_ref[...]
        probability = probability_ref[...]
        gate = jnp.sum(probability * chosen, axis=1, keepdims=True)
        half = buffer.shape[0] // n
        for i, ref in enumerate(refs[:n]):
            buffer[i * half : (i + 1) * half, :] = ref[:half, :]
        rows = dot(pack_ref[...], buffer[...])
        result_ref[...] = (middle + gate * rows).astype(jnp.bfloat16)
        gate_grad = jnp.sum(g * rows, axis=1, keepdims=True)
        logit_grad = (gate_grad * gate * (chosen - probability)).astype(jnp.bfloat16)
        router_part_ref[...] = dot(logit_grad, routed_ref[...], 0, 0)
        for i, ref in enumerate(refs[:n]):
            buffer[i * half : (i + 1) * half, :] = ref[half:, :]
        routed_grad = dot(logit_grad, router_ref[...]) + dot(pack_ref[...], buffer[...])
        spread = lax.rsqrt(jnp.mean(middle * middle, axis=1, keepdims=True) + 1e-06)
        gain_part_ref[...] = jnp.sum(routed_grad * middle * spread, axis=0, keepdims=True)
        u = routed_grad * gain_ref[...]
        mean = jnp.mean(u * middle, axis=1, keepdims=True)
        middle_grad = (g + spread * u - middle * (spread * spread * spread * mean)).astype(jnp.bfloat16)
        grad_out_ref[...] = middle_grad
        for m, o in zip(mixed_refs, ow_refs):
            m[...] = dot(middle_grad, o[...], 1, 1).astype(jnp.bfloat16)

    out = (
        shape((tokens, width)),
        shape((tokens, width)),
        shape(router.shape, jnp.float32),
        shape((1, width), jnp.float32),
    ) + (shape((tokens, hd)),) * shards
    args = (*back, pack_t, middle, routed, probability, chosen, grad, gain, router, *ow_pieces)
    scratch = [pltpu.VMEM((pack_t.shape[1], width), jnp.bfloat16)]
    return call(body, out, args, "token_grads", 0, scratch)


def cut_halves(part, bit, keep_ref, sent_ref):
    half = keep_ref.shape[0]
    keep_ref[...] = part[pl.ds(pl.multiple_of(bit * half, half), half), :]
    sent_ref[...] = part[pl.ds(pl.multiple_of((1 - bit) * half, half), half), :].astype(jnp.bfloat16)


def weight_part(head_ref, normed_ref, weight_refs, h, part, at):
    value = dot(head_ref[...], normed_ref[...])
    part[at : at + value.shape[0], :] = value
    size = value.shape[0] // 3
    gain = jnp.zeros((1, value.shape[1]), jnp.float32)
    for c, ref in enumerate(weight_refs):
        weight = ref[h * size : (h + 1) * size, :].astype(jnp.float32)
        gain = gain + jnp.sum(weight * value[c * size : (c + 1) * size, :], axis=0, keepdims=True)
    return gain


def place_grads(pieces, perm):
    tokens, hd = pieces[0].shape
    n = len(pieces)

    def body(*refs):
        perm_ref, out_ref = refs[n : n + 2]
        buffer = refs[-1]
        join(refs[:n], buffer)
        out_ref[...] = dot(buffer[...], perm_ref[...], 0, 0).astype(jnp.bfloat16)

    scratch = [pltpu.VMEM((n * tokens, hd), jnp.bfloat16)]
    return call(body, shape((hd, perm.shape[1])), (*pieces, perm), "place_grads", 0, scratch)


def first_parts(normed, head_grads, weights, middle_pieces, back, mixed_t, high):
    width = normed.shape[1]
    rows = head_grads[0].shape[0]
    n, hd = len(head_grads), mixed_t.shape[0]
    total = rows * n + hd

    def body(high_ref, normed_ref, wq_ref, wk_ref, wv_ref, back_ref, mixed_ref, *refs):
        keep_ref, sent_ref, gain_ref, middle_ref, part, buffer = refs[n + len(middle_pieces) :]
        gain = jnp.zeros(gain_ref.shape, jnp.float32)
        for h, ref in enumerate(refs[:n]):
            gain = gain + weight_part(ref, normed_ref, (wq_ref, wk_ref, wv_ref), h, part, h * rows)
        gain_ref[...] = gain
        join(refs[n : n + len(middle_pieces)], buffer)
        middle_ref[...] = dot(back_ref[...], buffer[...]).astype(jnp.bfloat16)
        part[n * rows :, :] = dot(mixed_ref[...], middle_ref[...])
        cut_halves(part, high_ref[0], keep_ref, sent_ref)

    out = (
        shape((total // 2, width), jnp.float32),
        shape((total // 2, width)),
        shape((1, width), jnp.float32),
        shape(normed.shape),
    )
    args = (normed, *weights, back, mixed_t, *head_grads, *middle_pieces)
    scratch = [pltpu.VMEM((total, width), jnp.float32), pltpu.VMEM((back.shape[1], width), jnp.bfloat16)]
    return with_bit(body, out, args, high, "first_parts", scratch)


def with_bit(body, out, args, high, name, scratch=()):
    return pl.pallas_call(
        body,
        out_shape=out,
        in_specs=[pl.BlockSpec(memory_space=pltpu.SMEM)] + in_vmem(len(args)),
        out_specs=jax.tree.map(lambda _: in_vmem(1)[0], out),
        scratch_shapes=list(scratch),
        compiler_params=pltpu.CompilerParams(vmem_limit_bytes=VMEM_LIMIT),
        cost_estimate=cost(name),
        name=name,
    )(high, *args)


def last_parts(normed, head_grad, weights, h, gain_before, gain, small, high):
    width = normed.shape[1]
    rows = head_grad.shape[0]
    total = rows + small.shape[0]

    def body(high_ref, normed_ref, head_ref, wq_ref, wk_ref, wv_ref, before_ref, gain_ref, small_ref, *refs):
        keep_ref, sent_ref, part = refs
        gain_part = weight_part(head_ref, normed_ref, (wq_ref, wk_ref, wv_ref), h, part, 0)
        line = lax.broadcasted_iota(jnp.int32, small_ref.shape, 0)
        gain_part = (before_ref[...] + gain_part) / gain_ref[...]
        part[rows:, :] = jnp.where(line == 0, gain_part, small_ref[...])
        cut_halves(part, high_ref[0], keep_ref, sent_ref)

    out = (shape((total // 2, width), jnp.float32), shape((total // 2, width)))
    args = (normed, head_grad, *weights, gain_before, gain, small)
    return with_bit(body, out, args, high, "last_parts", [pltpu.VMEM((total, width), jnp.float32)])


def place_sums(first, last, bits, heads, head_size):
    width = first[0].shape[1]
    hd = heads * head_size
    totals = (2 * first[0].shape[0], 2 * last[0].shape[0])

    def body(bits_ref, a0, a1, b0, b1, q_ref, k_ref, v_ref, o_ref, first_sum, last_sum):
        for i, (own, other, target) in enumerate(((a0, a1, first_sum), (b0, b1, last_sum))):
            half = own.shape[0]
            target[pl.ds(pl.multiple_of(bits_ref[i] * half, half), half), :] = own[...].astype(jnp.float32)
            target[pl.ds(pl.multiple_of((1 - bits_ref[i]) * half, half), half), :] = other[...].astype(jnp.float32)
        for h in range(heads):
            source, at = (first_sum, 3 * h * head_size) if h < heads - 1 else (last_sum, 0)
            for c, ref in enumerate((q_ref, k_ref, v_ref)):
                start = at + c * head_size
                ref[h * head_size : (h + 1) * head_size, :] = source[start : start + head_size, :]
        o_ref[...] = first_sum[3 * (heads - 1) * head_size :, :]

    out = (shape((hd, width), jnp.float32),) * 4
    scratch = [pltpu.VMEM((total, width), jnp.float32) for total in totals]
    return with_bit(body, out, (*first, *last), bits, "place_sums", scratch)


def place_halves(own, other, low):
    half, width = own.shape

    def body(low_ref, own_ref, other_ref, out_ref):
        out_ref[pl.ds(pl.multiple_of(low_ref[0] * half, half), half), :] = own_ref[...]
        out_ref[pl.ds(pl.multiple_of((1 - low_ref[0]) * half, half), half), :] = other_ref[...]

    return with_bit(body, shape((2 * half, width), own.dtype), (own, other), low.reshape(1), "place_halves")


def expert_weights(both_all, w_in, w_out):
    shards, _, count, width = both_all.shape

    def body(both_ref, wi_ref, wo_ref, in_ref, out_ref, rows_all, grads_all, hidden, before_grad):
        for s in range(shards):
            at = slice(s * count, (s + 1) * count)
            rows, grads = both_ref[s, 0], both_ref[s, 1]
            rows_all[at, :] = rows
            grads_all[at, :] = grads
            value, slope = gelu_pair(dot(rows, wi_ref[...]))
            hidden[at, :] = value.astype(jnp.bfloat16)
            before_grad[at, :] = (dot(grads, wo_ref[...], 1, 1) * slope).astype(jnp.bfloat16)
        in_ref[...] = dot(rows_all[...], before_grad[...], 0, 0)
        out_ref[...] = dot(hidden[...], grads_all[...], 0, 0)

    out = (shape(w_in.shape, jnp.float32), shape(w_out.shape, jnp.float32))
    scratch = [pltpu.VMEM((shards * count, n), jnp.bfloat16) for n in (width, width, w_in.shape[1], w_in.shape[1])]
    return call(body, out, (both_all, w_in, w_out), "expert_weights", 10**10, scratch)


def attention_backward_kernel(h, heads, head_size, rows, qkv_ref, bias_ref, grad_ref, out_ref, diag_ref, strip_ref, total_ref):
    length = qkv_ref.shape[1]
    blocks = length // rows
    hd = heads * head_size
    width = bias_ref.shape[1]
    strip_ref[...] = bias_strip(bias_ref[h : h + 1, :], rows)
    total_ref[...] = jnp.zeros_like(total_ref)
    qt32 = qkv_ref[h * head_size : (h + 1) * head_size, :].astype(jnp.float32) * 0.125
    qt = qt32.astype(jnp.bfloat16)
    q = qt32.T.astype(jnp.bfloat16)
    kt = qkv_ref[hd + h * head_size : hd + (h + 1) * head_size, :]
    k = kt.astype(jnp.float32).T.astype(jnp.bfloat16)
    vt = qkv_ref[2 * hd + h * head_size : 2 * hd + (h + 1) * head_size, :]
    gt = grad_ref[h * head_size : (h + 1) * head_size, :]
    g = gt.astype(jnp.float32).T.astype(jnp.bfloat16)
    dk = jnp.zeros((head_size, length), jnp.float32)
    dv = jnp.zeros((head_size, length), jnp.float32)
    for i in range(blocks):
        at = (blocks - 1 - i) * rows
        part = slice(i * rows, (i + 1) * rows)
        s = dot(q[part], kt) + strip_ref[:, at : at + length]
        peak = jnp.max(s, axis=1, keepdims=True)
        p = jnp.exp(s - peak)
        p = p * (1.0 / jnp.sum(p, axis=1, keepdims=True))
        dp = dot(g[part], vt)
        delta = jnp.sum(p * dp, axis=1, keepdims=True)
        ds = p * (dp - delta)
        total_ref[:, at : at + length] += ds
        dsb = ds.astype(jnp.bfloat16)
        dv = dv + dot(gt[:, part], p.astype(jnp.bfloat16))
        dk = dk + dot(qt[:, part], dsb)
        dq = dot(dsb, k) * 0.125
        out_ref[0:head_size, part] = dq.T.astype(jnp.bfloat16)
    out_ref[head_size : 2 * head_size, :] = dk.astype(jnp.bfloat16)
    out_ref[2 * head_size : 3 * head_size, :] = dv.astype(jnp.bfloat16)
    folded = total_ref[...]
    half = rows // 2
    while half:
        folded = folded[:half] + pltpu.roll(folded[half:], width - half, 1)
        half //= 2
    diag_ref[...] = pltpu.roll(folded, rows - 1, 1)


def attention_backward(qkv_t, bias_values, grad_t, h, heads, head_size, rows=256):
    length = qkv_t.shape[1]
    width = bias_values.shape[1]
    return pl.pallas_call(
        functools.partial(attention_backward_kernel, h, heads, head_size, rows),
        out_shape=(jax.ShapeDtypeStruct((3 * head_size, length), jnp.bfloat16), jax.ShapeDtypeStruct((1, width), jnp.float32)),
        in_specs=[pl.BlockSpec(memory_space=pltpu.VMEM)] * 3,
        out_specs=(pl.BlockSpec(memory_space=pltpu.VMEM),) * 2,
        scratch_shapes=[pltpu.VMEM((rows, width), jnp.float32)] * 2,
        compiler_params=pltpu.CompilerParams(vmem_limit_bytes=VMEM_LIMIT),
        cost_estimate=cost("attention_backward"),
        name="attention_backward",
    )(qkv_t, bias_values, grad_t)


def gelu_pair(v):
    inner = 0.7978845608028654 * (v + 0.044715 * v * v * v)
    t = jnp.tanh(inner)
    slope = 0.7978845608028654 * (1.0 + 3.0 * 0.044715 * v * v)
    return 0.5 * v * (1.0 + t), 0.5 * (1.0 + t) + 0.5 * v * (1.0 - t * t) * slope


def swap(x, axis, k):
    return lax.ppermute(x, axis, [(i, i ^ k) for i in range(lax.axis_size(axis))])


def gather_relative(x, axis="shard"):
    pieces = {0: x}
    bit = lax.axis_size(axis) // 2
    while bit:
        for k in sorted(pieces):
            pieces[k ^ bit] = swap(pieces[k], axis, bit)
        bit //= 2
    return [pieces[k] for k in range(len(pieces))]


def exchange_relative(pieces, axis):
    return [p if k == 0 else swap(p, axis, k) for k, p in enumerate(pieces)]


def exchange_window(pieces, axis, window):
    received = [pieces[0]]
    for k in range(1, len(pieces)):
        sent = pieces[k]
        if k > window:
            sent, received[k - window] = lax.optimization_barrier((sent, received[k - window]))
        received.append(swap(sent, axis, k))
    return received


def sum_pairs(x, axis):
    if lax.axis_size(axis) != 4:
        return lax.psum(x, axis)
    one, two, three = (swap(x, axis, k) for k in (1, 2, 3))
    return (x + one) + (two + three)


def sum_all(x, axis):
    if lax.axis_size(axis) > 8:
        return lax.psum(x, axis)
    bit = 1
    while bit < lax.axis_size(axis):
        x = x + swap(x, axis, bit)
        bit *= 2
    return x


def bit_of(me, bit):
    return (me & bit) // bit


def halving(keep, sent, axis, bits):
    me = lax.axis_index(axis)
    for i, bit in enumerate(bits):
        x = keep + (yield swap(sent, axis, bit)).astype(jnp.float32)
        if i + 1 < len(bits):
            half = x.shape[0] // 2
            high = bit_of(me, bits[i + 1])
            sent = lax.dynamic_slice_in_dim(x, (1 - high) * half, half, 0).astype(jnp.bfloat16)
            keep = lax.dynamic_slice_in_dim(x, high * half, half, 0)
    x = lax.optimization_barrier(x.astype(jnp.bfloat16))
    for bit in reversed(bits):
        other = yield swap(x, axis, bit)
        if bit != bits[0]:
            high = bit_of(me, bit)
            x = jnp.concatenate([jnp.where(high == 0, x, other), jnp.where(high == 0, other, x)], axis=0)
    yield x, other


def together(*arrays):
    return lax.optimization_barrier(arrays)


def on_device(
    inputs,
    cotangent,
    expert_id,
    slot_index,
    bucket_ids,
    attention_gain,
    query_weight,
    key_weight,
    value_weight,
    output_weight,
    bias_table,
    expert_gain,
    router_weight,
    expert_in,
    expert_out,
):
    bf16, f32 = jnp.bfloat16, jnp.float32
    length, width = inputs.shape
    buckets, heads = bias_table.shape
    hd = query_weight.shape[1]
    head_size = hd // heads
    experts = router_weight.shape[1]
    expert_devices = lax.axis_size("expert")
    shards = lax.axis_size("shard")
    me_e = lax.axis_index("expert")
    me_s = lax.axis_index("shard")
    part = max(1, 3 * length // (2 * experts * shards))
    owned = -(-(length + experts * (shards - 1)) // (16 * shards)) * 16
    relative = expert_devices <= 8
    w_in, w_out = expert_in[0], expert_out[0]

    sizes = [part] * expert_devices

    def exchange_experts(pieces, window):
        if relative:
            return exchange_window(pieces, "expert", window)
        blocks = jnp.stack(pieces)
        return list(lax.all_to_all(blocks, "expert", 0, 0))

    ow_pieces = gather_relative(output_weight)
    cut = w_in.shape[0] // 2
    far_top = swap(w_in[:cut], "shard", 2)

    w_rows = (query_weight.T, key_weight.T, value_weight.T)
    router_rows = router_weight.T

    residue = slot_index % shards
    group = slot_index // shards
    order = jnp.arange(length, dtype=jnp.int32)
    earlier = (order[None, :] < order[:, None]) & (residue[None, :] == residue[:, None])
    rank = jnp.sum(earlier.astype(jnp.int32), axis=1)
    place = (residue ^ me_s) * owned + rank
    numbers = jnp.arange(shards * owned, dtype=jnp.int32)[:, None]
    perm_flag = numbers == place[None, :]
    perm = lax.optimization_barrier(perm_flag.astype(bf16))
    own_flag = perm_flag[:owned]
    own = perm[:owned]

    def packing(expert):
        target = jnp.where(group < part, expert * part + group, -1)
        target_own = jnp.sum(jnp.where(own_flag, target[None, :] + 1, 0), axis=1) - 1
        numbers_own = jnp.arange(experts * part, dtype=jnp.int32)
        return (
            (numbers_own[:, None] == target_own[None, :]).astype(bf16),
            (numbers_own[None, :] == target_own[:, None]).astype(bf16),
        )

    pack, pack_t = packing(expert_id ^ me_e if relative else expert_id)
    expert_own = jnp.sum(jnp.where(own_flag, expert_id[None, :], 0), axis=1)

    offsets = jnp.concatenate([bucket_ids[1:, 0][::-1], bucket_ids[0, :], jnp.full((1,), -1, jnp.int32)])
    bucket_flag = offsets[None, :] == jnp.arange(buckets, dtype=jnp.int32)[:, None]
    bias_values = jnp.sum(jnp.where(bucket_flag[None], bias_table.T[:, :, None], 0.0), axis=1)
    mixed_t, qkv_t, normed = attention_forward(
        inputs, attention_gain[None, :], *w_rows, bias_values, heads, head_size
    )
    mixed_t, *ow_pieces = lax.optimization_barrier((mixed_t, *ow_pieces))
    mixed = dot(perm, mixed_t, 1, 1).astype(bf16)
    place, rank, mixed, cotangent, inputs_later, expert_gain, rest_in, rest_out = together(
        place, rank, mixed, cotangent, inputs, expert_gain, w_in[cut:], w_out
    )
    back = lax.optimization_barrier((place[:, None] == numbers.T).astype(bf16))
    back_absolute = lax.optimization_barrier(((residue * owned + rank)[:, None] == numbers.T).astype(bf16))
    mixed_own = exchange_relative([mixed[k * owned : (k + 1) * owned] for k in range(shards)], "shard")
    rest = jnp.concatenate([rest_in, rest_out], axis=0)
    source_own = dot(own, inputs_later)
    grad_own = dot(own, cotangent).astype(bf16)

    far_top, near_in, near_out, rest, *mixed_own = lax.optimization_barrier((far_top, w_in, w_out, rest, *mixed_own))
    far_rest = swap(rest, "shard", 2)
    near_in, near_out, last_top = swap(near_in, "shard", 1), swap(near_out, "shard", 1), swap(far_top, "shard", 1)

    middle, routed, probability, *pieces = route_tokens(
        mixed_own, ow_pieces, source_own, grad_own, pack, expert_gain[None, :], router_rows, sizes
    )
    near_in, near_out, last_top, *pieces = lax.optimization_barrier((near_in, near_out, last_top, *pieces))
    pieces = exchange_experts(pieces, 4)
    far_rest, *pieces = lax.optimization_barrier((far_rest, *pieces))
    last_rest = swap(far_rest, "shard", 1)

    mine = (jnp.arange(experts, dtype=jnp.int32)[None, :] == me_e).astype(f32)
    both, out_near, grad_near = expert_near(pieces, router_rows, mine, (w_in, w_out, near_in, near_out), part)
    both_all = lax.all_gather(both.reshape(2, expert_devices * part, width), "shard", axis=0)
    out_near, last_rest = lax.optimization_barrier((out_near, last_rest))
    far_all = (far_top, far_rest, last_top, last_rest)
    back_pieces = exchange_experts(expert_far(both, out_near, grad_near, far_all, part), 5)
    in_gradient, out_gradient = expert_weights(both_all, w_in, w_out)
    in_gradient, out_gradient, *back_pieces = together(in_gradient, out_gradient, *back_pieces)

    chosen = (expert_own[:, None] == jnp.arange(experts, dtype=jnp.int32)[None, :]).astype(f32)
    result_own, attention_grad, router_part, expert_gain_part, *mixed_grad = token_grads(
        back_pieces, pack_t, middle, routed, probability, chosen, grad_own, expert_gain[None, :],
        router_rows, ow_pieces,
    )
    mixed_grad = exchange_relative(mixed_grad, "shard")
    attention_grad, *mixed_grad = lax.optimization_barrier((attention_grad, *mixed_grad))
    far_grad, near_grad = swap(attention_grad, "shard", 2), swap(attention_grad, "shard", 1)
    mixed_grad_t = place_grads(mixed_grad, perm)

    w_heads = jnp.concatenate([w[h * head_size : (h + 1) * head_size] for h in range(heads) for w in w_rows], axis=0)
    bits = [1 << i for i in range(expert_devices.bit_length() - 1)]
    bits_first, bits_last = bits, [*bits[1:2], *bits[:1], *bits[2:]]
    high_first, high_last = bit_of(me_e, bits_first[0]).reshape(1), bit_of(me_e, bits_last[0]).reshape(1)
    head_grads, diagonals = [], []
    for h in range(heads):
        if h == heads - 1:
            keep_first, sent_first, gain_first, middle_grad_all = first_parts(
                normed, head_grads, w_rows, attention_grads, back, mixed_t, high_first
            )
            mixed_grad_t, sent_first, middle_grad_all = lax.optimization_barrier(
                (mixed_grad_t, sent_first, middle_grad_all)
            )
        head_grad, diagonal = attention_backward(qkv_t, bias_values, mixed_grad_t, h, heads, head_size)
        if h == 0:
            far_grad, near_grad, head_grad, result_own = together(far_grad, near_grad, head_grad, result_own)
            results = lax.all_gather(result_own, "shard", axis=0, tiled=True)
            attention_grads = [attention_grad, near_grad, far_grad, swap(far_grad, "shard", 1)]
        if h == heads - 1 and relative:
            sums_first = halving(keep_first, sent_first, "expert", bits_first)
            first, head_grad, diagonal = together(next(sums_first), head_grad, diagonal)
        head_grads.append(head_grad)
        diagonals.append(diagonal)
    qkv_grad_t = jnp.concatenate(head_grads, axis=0)

    normed_part = dot(qkv_grad_t, w_heads, 0, 0)
    half = length // 2
    low = me_s % 2
    other_half = lax.dynamic_slice_in_dim(normed_part, (1 - low) * half, half, 0)
    own_half = lax.dynamic_slice_in_dim(normed_part, low * half, half, 0)
    near_part = swap(other_half.astype(bf16), "shard", 1)
    if relative:
        first = sums_first.send(first)

    table_part = jnp.sum(jnp.where(bucket_flag[None], jnp.stack(diagonals), 0.0), axis=2).reshape(1, -1)
    table_part = jnp.pad(table_part, ((0, 0), (0, width - table_part.shape[1])))
    small = jnp.concatenate([jnp.zeros_like(table_part), expert_gain_part, router_part, table_part], axis=0)
    small = jnp.pad(small, ((0, -small.shape[0] % 64), (0, 0)))
    keep_last, sent_last = last_parts(
        normed, head_grads[-1], w_rows, heads - 1, gain_first, attention_gain[None, :], small, high_last
    )
    if relative:
        first, near_part, keep_last, results = together(first, near_part, keep_last, results)
        result = dot(back_absolute, results).astype(bf16)
        near_sum = (own_half + near_part.astype(f32)).astype(bf16)
        near_sum, sent_last = together(near_sum, sent_last)
        far_sum = swap(near_sum, "shard", 2)
        sums_last = halving(keep_last, sent_last, "expert", bits_last)
        first, last = together(sums_first.send(first), next(sums_last))
        for step in range(2 * len(bits) - 3):
            first, last = sums_first.send(first), sums_last.send(last)
            if step == 0:
                far_sum, first, last = together(far_sum, first, last)
            elif step == 1:
                result, first, last = together(result, first, last)
            else:
                first, last = together(first, last)
        first = sums_first.send(first)
        for _ in range(2):
            last = sums_last.send(last)
        last = sums_last.send(last)
    else:
        whole = []
        for keep, sent, high in ((keep_first, sent_first, high_first), (keep_last, sent_last, high_last)):
            sent = sent.astype(f32)
            low_part, high_part = jnp.where(high == 0, keep, sent), jnp.where(high == 0, sent, keep)
            low_part, high_part = lax.psum((low_part, high_part), "expert")
            whole.append((jnp.where(high == 0, low_part, high_part), jnp.where(high == 0, high_part, low_part)))
        first, last = whole
        near_sum = lax.optimization_barrier((own_half + near_part.astype(f32)).astype(bf16))
        far_sum = swap(near_sum, "shard", 2)
    if not relative:
        result = dot(back_absolute, results).astype(bf16)
    normed_grad = near_sum.astype(f32) + far_sum.astype(f32)
    source_half = lax.dynamic_slice_in_dim(inputs, low * half, half, 0).astype(f32)
    inverse_half = lax.rsqrt(jnp.mean(source_half * source_half, axis=-1, keepdims=True) + 1e-06)
    middle_half = lax.dynamic_slice_in_dim(middle_grad_all, low * half, half, 0).astype(f32)
    w = normed_grad * attention_gain
    grad_half = middle_half + inverse_half * w - source_half * (
        inverse_half * inverse_half * inverse_half * jnp.mean(w * source_half, axis=-1, keepdims=True)
    )
    grad_other = swap(grad_half, "shard", 1)
    input_gradient = place_halves(grad_half, grad_other, low)
    input_gradient, *last = together(input_gradient, *last)
    query_gradient, key_gradient, value_gradient, output_gradient = place_sums(
        first, last, jnp.concatenate([high_first, high_last]), heads, head_size
    )
    small = jnp.where(high_last == 0, last[1], last[0])[last[0].shape[0] - small.shape[0] :].astype(f32)
    table_gradient = small[2 + experts, : buckets * heads].reshape(heads, buckets).T
    small = sum_pairs(small[: 2 + experts], "shard")

    return (
        result,
        input_gradient,
        small[0],
        query_gradient.T,
        key_gradient.T,
        value_gradient.T,
        output_gradient,
        table_gradient,
        small[1],
        small[2:].T,
        in_gradient[None],
        out_gradient[None],
    )


def solution(mesh):
    placed = (
        P("expert", None),
        P("expert", None),
        P("expert"),
        P("expert"),
        P(),
        P(),
        P(None, "shard"),
        P(None, "shard"),
        P(None, "shard"),
        P("shard", None),
        P(None, "shard"),
        P(),
        P(),
        P("expert", None, "shard"),
        P("expert", "shard", None),
    )
    return jax.shard_map(
        on_device,
        mesh=mesh,
        in_specs=placed,
        out_specs=(
            P("expert", None),
            P("expert", None),
            P(),
            P(None, "shard"),
            P(None, "shard"),
            P(None, "shard"),
            P("shard", None),
            P(None, "shard"),
            P(),
            P(),
            P("expert", None, "shard"),
            P("expert", "shard", None),
        ),
        check_vma=False,
    )
```

```python
import functools
import jax
import jax.numpy as jnp
from jax import lax
from jax.experimental import pallas as pl
from jax.experimental.pallas import tpu as pltpu
from jax.sharding import PartitionSpec as P

TIMES = {"attention_forward": 9.4, "attention_backward": 6.7, "route_tokens": 4.7, "expert_near": 8.4, "expert_far": 9.6, "token_grads": 5.0, "first_parts": 8.0, "last_parts": 3.2, "place_sums": 2.9, "place_halves": 3.8, "expert_weights": 14.3, "place_grads": 3.4}


def cost(name):
    return pl.CostEstimate(flops=int(TIMES[name] * 1.15e9), bytes_accessed=10**5, transcendentals=0)


VMEM_LIMIT = 56 * 1024 * 1024


def dot(a, b, ca=1, cb=0):
    return lax.dot_general(a, b, (((ca,), (cb,)), ((), ())), preferred_element_type=jnp.float32)


def bias_strip(values_row, rows):
    total = values_row.shape[-1]
    wide = jnp.broadcast_to(values_row.reshape(1, total), (rows, total))
    return pltpu.roll(wide, total - rows + 1, 1, stride=1, stride_axis=0)


def attention_forward_kernel(heads, head_size, rows, in_ref, gain_ref, wq_ref, wk_ref, wv_ref, bias_ref, mixed_ref, qkv_ref, normed_ref, strip_ref):
    length = in_ref.shape[0]
    blocks = length // rows
    hd = heads * head_size
    source = in_ref[...].astype(jnp.float32)
    inverse = lax.rsqrt(jnp.mean(source * source, axis=1, keepdims=True) + 1e-06)
    normed_ref[...] = (source * inverse * gain_ref[...]).astype(jnp.bfloat16)
    for at, ref in enumerate((wq_ref, wk_ref, wv_ref)):
        qkv_ref[at * hd : (at + 1) * hd, :] = dot(ref[...], normed_ref[...], 1, 1).astype(jnp.bfloat16)
    for h in range(heads):
        strip_ref[...] = bias_strip(bias_ref[h : h + 1, :], rows)
        q = (qkv_ref[h * head_size : (h + 1) * head_size, :].astype(jnp.float32) * 0.125).T.astype(jnp.bfloat16)
        kt = qkv_ref[hd + h * head_size : hd + (h + 1) * head_size, :]
        vt = qkv_ref[2 * hd + h * head_size : 2 * hd + (h + 1) * head_size, :]
        for i in range(blocks):
            s = dot(q[i * rows : (i + 1) * rows], kt)
            at = (blocks - 1 - i) * rows
            s = s + strip_ref[:, at : at + length]
            peak = jnp.max(s, axis=1, keepdims=True)
            p = jnp.exp(s - peak)
            total = jnp.sum(p, axis=1, keepdims=True)
            o = dot(p.astype(jnp.bfloat16), vt, 1, 1) / total
            mixed_ref[h * head_size : (h + 1) * head_size, i * rows : (i + 1) * rows] = o.T.astype(jnp.bfloat16)


def in_vmem(count):
    return [pl.BlockSpec(memory_space=pltpu.VMEM)] * count


def attention_forward(inputs, gain, wq, wk, wv, bias_values, heads, head_size, rows=256):
    length = inputs.shape[0]
    hd = heads * head_size
    return pl.pallas_call(
        functools.partial(attention_forward_kernel, heads, head_size, rows),
        out_shape=(
            jax.ShapeDtypeStruct((hd, length), jnp.bfloat16),
            jax.ShapeDtypeStruct((3 * hd, length), jnp.bfloat16),
            jax.ShapeDtypeStruct(inputs.shape, jnp.bfloat16),
        ),
        in_specs=in_vmem(6),
        out_specs=tuple(in_vmem(3)),
        scratch_shapes=[pltpu.VMEM((rows, bias_values.shape[1]), jnp.float32)],
        compiler_params=pltpu.CompilerParams(vmem_limit_bytes=VMEM_LIMIT),
        cost_estimate=cost("attention_forward"),
        name="attention_forward",
    )(inputs, gain, wq, wk, wv, bias_values)


def call(body, out_shape, args, name, flops, scratch=(), transcendentals=0):
    return pl.pallas_call(
        body,
        out_shape=out_shape,
        in_specs=in_vmem(len(args)),
        out_specs=jax.tree.map(lambda _: in_vmem(1)[0], out_shape),
        scratch_shapes=list(scratch),
        compiler_params=pltpu.CompilerParams(vmem_limit_bytes=VMEM_LIMIT),
        cost_estimate=cost(name),
        name=name,
    )(*args)


def shape(dims, dtype=jnp.bfloat16):
    return jax.ShapeDtypeStruct(dims, dtype)


def join(refs, target):
    at = 0
    for ref in refs:
        target[at : at + ref.shape[0], :] = ref[...]
        at += ref.shape[0]


def route_tokens(mixed_pieces, ow_pieces, source, grad, pack, gain, router, sizes):
    shards = len(mixed_pieces)
    tokens, width = source.shape

    def body(*refs):
        mixed_refs, ow_refs = refs[:shards], refs[shards : 2 * shards]
        source_ref, grad_ref, pack_ref, gain_ref, router_ref = refs[2 * shards : 2 * shards + 5]
        middle_ref, routed_ref, probability_ref = refs[2 * shards + 5 : 2 * shards + 8]
        middle = source_ref[...]
        for m, o in zip(mixed_refs, ow_refs):
            middle = middle + dot(m[...], o[...])
        middle_ref[...] = middle
        spread = lax.rsqrt(jnp.mean(middle * middle, axis=1, keepdims=True) + 1e-06)
        routed = (middle * spread * gain_ref[...]).astype(jnp.bfloat16)
        routed_ref[...] = routed
        packed = dot(pack_ref[...], routed).astype(jnp.bfloat16)
        packed_grad = dot(pack_ref[...], grad_ref[...]).astype(jnp.bfloat16)
        at = 0
        for ref in refs[2 * shards + 8 :]:
            size = ref.shape[0] // 2
            ref[:size, :] = packed[at : at + size, :]
            ref[size:, :] = packed_grad[at : at + size, :]
            at += size
        logits = dot(routed, router_ref[...], 1, 1)
        powered = jnp.exp(logits - jnp.max(logits, axis=1, keepdims=True))
        probability_ref[...] = powered / jnp.sum(powered, axis=1, keepdims=True)

    out = (shape((tokens, width), jnp.float32), shape((tokens, width)), shape((tokens, router.shape[0]), jnp.float32))
    out = out + tuple(shape((2 * n, width)) for n in sizes)
    args = (*mixed_pieces, *ow_pieces, source, grad, pack, gain, router)
    return call(body, out, args, "route_tokens", 0)


def gated(rows, grads, router, mine):
    logits = dot(rows, router, 1, 1)
    powered = jnp.exp(logits - jnp.max(logits, axis=1, keepdims=True))
    gate = jnp.sum(powered * mine, axis=1, keepdims=True) / jnp.sum(powered, axis=1, keepdims=True)
    return (gate * grads.astype(jnp.float32)).astype(jnp.bfloat16)


def expert_units(rows, grads, in_parts, out, out_ref, grad_ref):
    at, before = 0, 0.0
    for part in in_parts:
        before = before + dot(rows[:, at : at + part.shape[0]], part)
        at += part.shape[0]
    value, slope = gelu_pair(before)
    out_ref[...] += dot(value.astype(jnp.bfloat16), out)
    before_grad = (dot(grads, out, 1, 1) * slope).astype(jnp.bfloat16)
    at = 0
    for part in in_parts:
        grad_ref[:, at : at + part.shape[0]] += dot(before_grad, part, 1, 1)
        at += part.shape[0]


def expert_near(pieces, router, mine, weights, part):
    count, width = part * len(pieces), pieces[0].shape[1]
    n = len(pieces)

    def body(*refs):
        router_ref, mine_ref, in0, out0, in1, out1, both_ref, out_ref, grad_ref = refs[n:]
        for i, ref in enumerate(refs[:n]):
            both_ref[i * part : (i + 1) * part, :] = ref[:part, :]
            both_ref[count + i * part : count + (i + 1) * part, :] = ref[part:, :]
        rows = both_ref[:count, :]
        both_ref[count:, :] = gated(rows, both_ref[count:, :], router_ref[...], mine_ref[...])
        out_ref[...] = jnp.zeros_like(out_ref)
        grad_ref[...] = jnp.zeros_like(grad_ref)
        for i, o in ((in0, out0), (in1, out1)):
            expert_units(rows, both_ref[count:, :], (i[...],), o[...], out_ref, grad_ref)

    out = (shape((2 * count, width)), shape((count, width), jnp.float32), shape((count, width), jnp.float32))
    return call(body, out, (*pieces, router, mine, *weights), "expert_near", 0)


def expert_far(both, out_before, grad_before, weights, part):
    count, width = out_before.shape

    def body(both_ref, out_ref, grad_ref, top0, rest0, top1, rest1, *refs):
        out_total, grad_total = refs[-2:]
        out_total[...] = out_ref[...]
        grad_total[...] = grad_ref[...]
        for top, rest in ((top0, rest0), (top1, rest1)):
            cut = width - top.shape[0]
            in_parts = (top[...], rest[:cut, :])
            expert_units(both_ref[:count, :], both_ref[count:, :], in_parts, rest[cut:, :], out_total, grad_total)
        for i, ref in enumerate(refs[:-2]):
            ref[:part, :] = out_total[i * part : (i + 1) * part, :].astype(jnp.bfloat16)
            ref[part:, :] = grad_total[i * part : (i + 1) * part, :].astype(jnp.bfloat16)

    out = tuple(shape((2 * part, width)) for _ in range(count // part))
    scratch = [pltpu.VMEM((count, width), jnp.float32)] * 2
    return list(call(body, out, (both, out_before, grad_before, *weights), "expert_far", 0, scratch))


def token_grads(back, pack_t, middle, routed, probability, chosen, grad, gain, router, ow_pieces):
    tokens, width = middle.shape
    n, shards = len(back), len(ow_pieces)
    hd = ow_pieces[0].shape[0]

    def body(*refs):
        pack_ref, middle_ref, routed_ref, probability_ref, chosen_ref, g_ref, gain_ref, router_ref = refs[n : n + 8]
        ow_refs = refs[n + 8 : n + 8 + shards]
        result_ref, grad_out_ref, router_part_ref, gain_part_ref = refs[n + 8 + shards : n + 12 + shards]
        mixed_refs = refs[n + 12 + shards : n + 12 + 2 * shards]
        buffer = refs[-1]
        g = g_ref[...].astype(jnp.float32)
        middle = middle_ref[...]
        chosen = chosen_ref[...]
        probability = probability_ref[...]
        gate = jnp.sum(probability * chosen, axis=1, keepdims=True)
        half = buffer.shape[0] // n
        for i, ref in enumerate(refs[:n]):
            buffer[i * half : (i + 1) * half, :] = ref[:half, :]
        rows = dot(pack_ref[...], buffer[...])
        result_ref[...] = (middle + gate * rows).astype(jnp.bfloat16)
        gate_grad = jnp.sum(g * rows, axis=1, keepdims=True)
        logit_grad = (gate_grad * gate * (chosen - probability)).astype(jnp.bfloat16)
        router_part_ref[...] = dot(logit_grad, routed_ref[...], 0, 0)
        for i, ref in enumerate(refs[:n]):
            buffer[i * half : (i + 1) * half, :] = ref[half:, :]
        routed_grad = dot(logit_grad, router_ref[...]) + dot(pack_ref[...], buffer[...])
        spread = lax.rsqrt(jnp.mean(middle * middle, axis=1, keepdims=True) + 1e-06)
        gain_part_ref[...] = jnp.sum(routed_grad * middle * spread, axis=0, keepdims=True)
        u = routed_grad * gain_ref[...]
        mean = jnp.mean(u * middle, axis=1, keepdims=True)
        middle_grad = (g + spread * u - middle * (spread * spread * spread * mean)).astype(jnp.bfloat16)
        grad_out_ref[...] = middle_grad
        for m, o in zip(mixed_refs, ow_refs):
            m[...] = dot(middle_grad, o[...], 1, 1).astype(jnp.bfloat16)

    out = (
        shape((tokens, width)),
        shape((tokens, width)),
        shape(router.shape, jnp.float32),
        shape((1, width), jnp.float32),
    ) + (shape((tokens, hd)),) * shards
    args = (*back, pack_t, middle, routed, probability, chosen, grad, gain, router, *ow_pieces)
    scratch = [pltpu.VMEM((pack_t.shape[1], width), jnp.bfloat16)]
    return call(body, out, args, "token_grads", 0, scratch)


def cut_halves(part, bit, keep_ref, sent_ref):
    half = keep_ref.shape[0]
    keep_ref[...] = part[pl.ds(pl.multiple_of(bit * half, half), half), :]
    sent_ref[...] = part[pl.ds(pl.multiple_of((1 - bit) * half, half), half), :].astype(jnp.bfloat16)


def weight_part(head_ref, normed_ref, weight_refs, h, part, at):
    value = dot(head_ref[...], normed_ref[...])
    part[at : at + value.shape[0], :] = value
    size = value.shape[0] // 3
    gain = jnp.zeros((1, value.shape[1]), jnp.float32)
    for c, ref in enumerate(weight_refs):
        weight = ref[h * size : (h + 1) * size, :].astype(jnp.float32)
        gain = gain + jnp.sum(weight * value[c * size : (c + 1) * size, :], axis=0, keepdims=True)
    return gain


def place_grads(pieces, perm):
    tokens, hd = pieces[0].shape
    n = len(pieces)

    def body(*refs):
        perm_ref, out_ref = refs[n : n + 2]
        buffer = refs[-1]
        join(refs[:n], buffer)
        out_ref[...] = dot(buffer[...], perm_ref[...], 0, 0).astype(jnp.bfloat16)

    scratch = [pltpu.VMEM((n * tokens, hd), jnp.bfloat16)]
    return call(body, shape((hd, perm.shape[1])), (*pieces, perm), "place_grads", 0, scratch)


def first_parts(normed, head_grads, weights, middle_pieces, back, mixed_t, high):
    width = normed.shape[1]
    rows = head_grads[0].shape[0]
    n, hd = len(head_grads), mixed_t.shape[0]
    total = rows * n + hd

    def body(high_ref, normed_ref, wq_ref, wk_ref, wv_ref, back_ref, mixed_ref, *refs):
        keep_ref, sent_ref, gain_ref, middle_ref, part, buffer = refs[n + len(middle_pieces) :]
        gain = jnp.zeros(gain_ref.shape, jnp.float32)
        for h, ref in enumerate(refs[:n]):
            gain = gain + weight_part(ref, normed_ref, (wq_ref, wk_ref, wv_ref), h, part, h * rows)
        gain_ref[...] = gain
        join(refs[n : n + len(middle_pieces)], buffer)
        middle_ref[...] = dot(back_ref[...], buffer[...]).astype(jnp.bfloat16)
        part[n * rows :, :] = dot(mixed_ref[...], middle_ref[...])
        cut_halves(part, high_ref[0], keep_ref, sent_ref)

    out = (
        shape((total // 2, width), jnp.float32),
        shape((total // 2, width)),
        shape((1, width), jnp.float32),
        shape(normed.shape),
    )
    args = (normed, *weights, back, mixed_t, *head_grads, *middle_pieces)
    scratch = [pltpu.VMEM((total, width), jnp.float32), pltpu.VMEM((back.shape[1], width), jnp.bfloat16)]
    return with_bit(body, out, args, high, "first_parts", scratch)


def with_bit(body, out, args, high, name, scratch=()):
    return pl.pallas_call(
        body,
        out_shape=out,
        in_specs=[pl.BlockSpec(memory_space=pltpu.SMEM)] + in_vmem(len(args)),
        out_specs=jax.tree.map(lambda _: in_vmem(1)[0], out),
        scratch_shapes=list(scratch),
        compiler_params=pltpu.CompilerParams(vmem_limit_bytes=VMEM_LIMIT),
        cost_estimate=cost(name),
        name=name,
    )(high, *args)


def last_parts(normed, head_grad, weights, h, gain_before, gain, small, high):
    width = normed.shape[1]
    rows = head_grad.shape[0]
    total = rows + small.shape[0]

    def body(high_ref, normed_ref, head_ref, wq_ref, wk_ref, wv_ref, before_ref, gain_ref, small_ref, *refs):
        keep_ref, sent_ref, part = refs
        gain_part = weight_part(head_ref, normed_ref, (wq_ref, wk_ref, wv_ref), h, part, 0)
        line = lax.broadcasted_iota(jnp.int32, small_ref.shape, 0)
        gain_part = (before_ref[...] + gain_part) / gain_ref[...]
        part[rows:, :] = jnp.where(line == 0, gain_part, small_ref[...])
        cut_halves(part, high_ref[0], keep_ref, sent_ref)

    out = (shape((total // 2, width), jnp.float32), shape((total // 2, width)))
    args = (normed, head_grad, *weights, gain_before, gain, small)
    return with_bit(body, out, args, high, "last_parts", [pltpu.VMEM((total, width), jnp.float32)])


def place_sums(first, last, bits, heads, head_size):
    width = first[0].shape[1]
    hd = heads * head_size
    totals = (2 * first[0].shape[0], 2 * last[0].shape[0])

    def body(bits_ref, a0, a1, b0, b1, q_ref, k_ref, v_ref, o_ref, first_sum, last_sum):
        for i, (own, other, target) in enumerate(((a0, a1, first_sum), (b0, b1, last_sum))):
            half = own.shape[0]
            target[pl.ds(pl.multiple_of(bits_ref[i] * half, half), half), :] = own[...].astype(jnp.float32)
            target[pl.ds(pl.multiple_of((1 - bits_ref[i]) * half, half), half), :] = other[...].astype(jnp.float32)
        for h in range(heads):
            source, at = (first_sum, 3 * h * head_size) if h < heads - 1 else (last_sum, 0)
            for c, ref in enumerate((q_ref, k_ref, v_ref)):
                start = at + c * head_size
                ref[h * head_size : (h + 1) * head_size, :] = source[start : start + head_size, :]
        o_ref[...] = first_sum[3 * (heads - 1) * head_size :, :]

    out = (shape((hd, width), jnp.float32),) * 4
    scratch = [pltpu.VMEM((total, width), jnp.float32) for total in totals]
    return with_bit(body, out, (*first, *last), bits, "place_sums", scratch)


def place_halves(own, other, low):
    half, width = own.shape

    def body(low_ref, own_ref, other_ref, out_ref):
        out_ref[pl.ds(pl.multiple_of(low_ref[0] * half, half), half), :] = own_ref[...]
        out_ref[pl.ds(pl.multiple_of((1 - low_ref[0]) * half, half), half), :] = other_ref[...]

    return with_bit(body, shape((2 * half, width), own.dtype), (own, other), low.reshape(1), "place_halves")


def expert_weights(both_all, w_in, w_out):
    shards, _, count, width = both_all.shape

    def body(both_ref, wi_ref, wo_ref, in_ref, out_ref, rows_all, grads_all, hidden, before_grad):
        for s in range(shards):
            at = slice(s * count, (s + 1) * count)
            rows, grads = both_ref[s, 0], both_ref[s, 1]
            rows_all[at, :] = rows
            grads_all[at, :] = grads
            value, slope = gelu_pair(dot(rows, wi_ref[...]))
            hidden[at, :] = value.astype(jnp.bfloat16)
            before_grad[at, :] = (dot(grads, wo_ref[...], 1, 1) * slope).astype(jnp.bfloat16)
        in_ref[...] = dot(rows_all[...], before_grad[...], 0, 0)
        out_ref[...] = dot(hidden[...], grads_all[...], 0, 0)

    out = (shape(w_in.shape, jnp.float32), shape(w_out.shape, jnp.float32))
    scratch = [pltpu.VMEM((shards * count, n), jnp.bfloat16) for n in (width, width, w_in.shape[1], w_in.shape[1])]
    return call(body, out, (both_all, w_in, w_out), "expert_weights", 10**10, scratch)


def attention_backward_kernel(h, heads, head_size, rows, qkv_ref, bias_ref, grad_ref, out_ref, diag_ref, strip_ref, total_ref):
    length = qkv_ref.shape[1]
    blocks = length // rows
    hd = heads * head_size
    width = bias_ref.shape[1]
    strip_ref[...] = bias_strip(bias_ref[h : h + 1, :], rows)
    total_ref[...] = jnp.zeros_like(total_ref)
    qt32 = qkv_ref[h * head_size : (h + 1) * head_size, :].astype(jnp.float32) * 0.125
    qt = qt32.astype(jnp.bfloat16)
    q = qt32.T.astype(jnp.bfloat16)
    kt = qkv_ref[hd + h * head_size : hd + (h + 1) * head_size, :]
    k = kt.astype(jnp.float32).T.astype(jnp.bfloat16)
    vt = qkv_ref[2 * hd + h * head_size : 2 * hd + (h + 1) * head_size, :]
    gt = grad_ref[h * head_size : (h + 1) * head_size, :]
    g = gt.astype(jnp.float32).T.astype(jnp.bfloat16)
    dk = jnp.zeros((head_size, length), jnp.float32)
    dv = jnp.zeros((head_size, length), jnp.float32)
    for i in range(blocks):
        at = (blocks - 1 - i) * rows
        part = slice(i * rows, (i + 1) * rows)
        s = dot(q[part], kt) + strip_ref[:, at : at + length]
        peak = jnp.max(s, axis=1, keepdims=True)
        p = jnp.exp(s - peak)
        p = p * (1.0 / jnp.sum(p, axis=1, keepdims=True))
        dp = dot(g[part], vt)
        delta = jnp.sum(p * dp, axis=1, keepdims=True)
        ds = p * (dp - delta)
        total_ref[:, at : at + length] += ds
        dsb = ds.astype(jnp.bfloat16)
        dv = dv + dot(gt[:, part], p.astype(jnp.bfloat16))
        dk = dk + dot(qt[:, part], dsb)
        dq = dot(dsb, k) * 0.125
        out_ref[0:head_size, part] = dq.T.astype(jnp.bfloat16)
    out_ref[head_size : 2 * head_size, :] = dk.astype(jnp.bfloat16)
    out_ref[2 * head_size : 3 * head_size, :] = dv.astype(jnp.bfloat16)
    folded = total_ref[...]
    half = rows // 2
    while half:
        folded = folded[:half] + pltpu.roll(folded[half:], width - half, 1)
        half //= 2
    diag_ref[...] = pltpu.roll(folded, rows - 1, 1)


def attention_backward(qkv_t, bias_values, grad_t, h, heads, head_size, rows=256):
    length = qkv_t.shape[1]
    width = bias_values.shape[1]
    return pl.pallas_call(
        functools.partial(attention_backward_kernel, h, heads, head_size, rows),
        out_shape=(jax.ShapeDtypeStruct((3 * head_size, length), jnp.bfloat16), jax.ShapeDtypeStruct((1, width), jnp.float32)),
        in_specs=[pl.BlockSpec(memory_space=pltpu.VMEM)] * 3,
        out_specs=(pl.BlockSpec(memory_space=pltpu.VMEM),) * 2,
        scratch_shapes=[pltpu.VMEM((rows, width), jnp.float32)] * 2,
        compiler_params=pltpu.CompilerParams(vmem_limit_bytes=VMEM_LIMIT),
        cost_estimate=cost("attention_backward"),
        name="attention_backward",
    )(qkv_t, bias_values, grad_t)


def gelu_pair(v):
    inner = 0.7978845608028654 * (v + 0.044715 * v * v * v)
    t = jnp.tanh(inner)
    slope = 0.7978845608028654 * (1.0 + 3.0 * 0.044715 * v * v)
    return 0.5 * v * (1.0 + t), 0.5 * (1.0 + t) + 0.5 * v * (1.0 - t * t) * slope


def swap(x, axis, k):
    return lax.ppermute(x, axis, [(i, i ^ k) for i in range(lax.axis_size(axis))])


def gather_relative(x, axis="shard"):
    pieces = {0: x}
    bit = lax.axis_size(axis) // 2
    while bit:
        for k in sorted(pieces):
            pieces[k ^ bit] = swap(pieces[k], axis, bit)
        bit //= 2
    return [pieces[k] for k in range(len(pieces))]


def exchange_relative(pieces, axis):
    return [p if k == 0 else swap(p, axis, k) for k, p in enumerate(pieces)]


def exchange_window(pieces, axis, window):
    received = [pieces[0]]
    for k in range(1, len(pieces)):
        sent = pieces[k]
        if k > window:
            sent, received[k - window] = lax.optimization_barrier((sent, received[k - window]))
        received.append(swap(sent, axis, k))
    return received


def sum_pairs(x, axis):
    if lax.axis_size(axis) != 4:
        return lax.psum(x, axis)
    one, two, three = (swap(x, axis, k) for k in (1, 2, 3))
    return (x + one) + (two + three)


def sum_all(x, axis):
    if lax.axis_size(axis) > 8:
        return lax.psum(x, axis)
    bit = 1
    while bit < lax.axis_size(axis):
        x = x + swap(x, axis, bit)
        bit *= 2
    return x


def bit_of(me, bit):
    return (me & bit) // bit


def halving(keep, sent, axis, bits):
    me = lax.axis_index(axis)
    for i, bit in enumerate(bits):
        x = keep + (yield swap(sent, axis, bit)).astype(jnp.float32)
        if i + 1 < len(bits):
            half = x.shape[0] // 2
            high = bit_of(me, bits[i + 1])
            sent = lax.dynamic_slice_in_dim(x, (1 - high) * half, half, 0).astype(jnp.bfloat16)
            keep = lax.dynamic_slice_in_dim(x, high * half, half, 0)
    x = lax.optimization_barrier(x.astype(jnp.bfloat16))
    for bit in reversed(bits):
        other = yield swap(x, axis, bit)
        if bit != bits[0]:
            high = bit_of(me, bit)
            x = jnp.concatenate([jnp.where(high == 0, x, other), jnp.where(high == 0, other, x)], axis=0)
    yield x, other


def together(*arrays):
    return lax.optimization_barrier(arrays)


def on_device(
    inputs,
    cotangent,
    expert_id,
    slot_index,
    bucket_ids,
    attention_gain,
    query_weight,
    key_weight,
    value_weight,
    output_weight,
    bias_table,
    expert_gain,
    router_weight,
    expert_in,
    expert_out,
):
    bf16, f32 = jnp.bfloat16, jnp.float32
    length, width = inputs.shape
    buckets, heads = bias_table.shape
    hd = query_weight.shape[1]
    head_size = hd // heads
    experts = router_weight.shape[1]
    expert_devices = lax.axis_size("expert")
    shards = lax.axis_size("shard")
    me_e = lax.axis_index("expert")
    me_s = lax.axis_index("shard")
    part = max(1, 3 * length // (2 * experts * shards))
    owned = -(-(length + experts * (shards - 1)) // (16 * shards)) * 16
    relative = expert_devices <= 8
    w_in, w_out = expert_in[0], expert_out[0]

    sizes = [part] * expert_devices

    def exchange_experts(pieces, window):
        if relative:
            return exchange_window(pieces, "expert", window)
        blocks = jnp.stack(pieces)
        return list(lax.all_to_all(blocks, "expert", 0, 0))

    ow_pieces = gather_relative(output_weight)
    cut = w_in.shape[0] // 2
    far_top = swap(w_in[:cut], "shard", 2)

    w_rows = (query_weight.T, key_weight.T, value_weight.T)
    router_rows = router_weight.T

    residue = slot_index % shards
    group = slot_index // shards
    order = jnp.arange(length, dtype=jnp.int32)
    earlier = (order[None, :] < order[:, None]) & (residue[None, :] == residue[:, None])
    rank = jnp.sum(earlier.astype(jnp.int32), axis=1)
    place = (residue ^ me_s) * owned + rank
    numbers = jnp.arange(shards * owned, dtype=jnp.int32)[:, None]
    perm_flag = numbers == place[None, :]
    perm = lax.optimization_barrier(perm_flag.astype(bf16))
    own_flag = perm_flag[:owned]
    own = perm[:owned]

    def packing(expert):
        target = jnp.where(group < part, expert * part + group, -1)
        target_own = jnp.sum(jnp.where(own_flag, target[None, :] + 1, 0), axis=1) - 1
        numbers_own = jnp.arange(experts * part, dtype=jnp.int32)
        return (
            (numbers_own[:, None] == target_own[None, :]).astype(bf16),
            (numbers_own[None, :] == target_own[:, None]).astype(bf16),
        )

    pack, pack_t = packing(expert_id ^ me_e if relative else expert_id)
    expert_own = jnp.sum(jnp.where(own_flag, expert_id[None, :], 0), axis=1)

    offsets = jnp.concatenate([bucket_ids[1:, 0][::-1], bucket_ids[0, :], jnp.full((1,), -1, jnp.int32)])
    bucket_flag = offsets[None, :] == jnp.arange(buckets, dtype=jnp.int32)[:, None]
    bias_values = jnp.sum(jnp.where(bucket_flag[None], bias_table.T[:, :, None], 0.0), axis=1)
    mixed_t, qkv_t, normed = attention_forward(
        inputs, attention_gain[None, :], *w_rows, bias_values, heads, head_size
    )
    mixed_t, *ow_pieces = lax.optimization_barrier((mixed_t, *ow_pieces))
    mixed = dot(perm, mixed_t, 1, 1).astype(bf16)
    place, rank, mixed, cotangent, inputs_later, expert_gain, rest_in, rest_out = together(
        place, rank, mixed, cotangent, inputs, expert_gain, w_in[cut:], w_out
    )
    back = lax.optimization_barrier((place[:, None] == numbers.T).astype(bf16))
    back_absolute = lax.optimization_barrier(((residue * owned + rank)[:, None] == numbers.T).astype(bf16))
    mixed_own = exchange_relative([mixed[k * owned : (k + 1) * owned] for k in range(shards)], "shard")
    rest = jnp.concatenate([rest_in, rest_out], axis=0)
    source_own = dot(own, inputs_later)
    grad_own = dot(own, cotangent).astype(bf16)

    far_top, near_in, near_out, rest, *mixed_own = lax.optimization_barrier((far_top, w_in, w_out, rest, *mixed_own))
    far_rest = swap(rest, "shard", 2)
    near_in, near_out, last_top = swap(near_in, "shard", 1), swap(near_out, "shard", 1), swap(far_top, "shard", 1)

    middle, routed, probability, *pieces = route_tokens(
        mixed_own, ow_pieces, source_own, grad_own, pack, expert_gain[None, :], router_rows, sizes
    )
    near_in, near_out, last_top, *pieces = lax.optimization_barrier((near_in, near_out, last_top, *pieces))
    pieces = exchange_experts(pieces, 4)
    far_rest, pieces[-1] = together(far_rest, pieces[-1])
    last_rest = swap(far_rest, "shard", 1)

    mine = (jnp.arange(experts, dtype=jnp.int32)[None, :] == me_e).astype(f32)
    both, out_near, grad_near = expert_near(pieces, router_rows, mine, (w_in, w_out, near_in, near_out), part)
    both, out_near, last_rest = together(both, out_near, last_rest)
    both_all = lax.all_gather(both.reshape(2, expert_devices * part, width), "shard", axis=0)
    far_all = (far_top, far_rest, last_top, last_rest)
    back_pieces = exchange_experts(expert_far(both, out_near, grad_near, far_all, part), 5)
    in_gradient, out_gradient = expert_weights(both_all, w_in, w_out)
    in_gradient, out_gradient, *back_pieces = together(in_gradient, out_gradient, *back_pieces)

    chosen = (expert_own[:, None] == jnp.arange(experts, dtype=jnp.int32)[None, :]).astype(f32)
    result_own, attention_grad, router_part, expert_gain_part, *mixed_grad = token_grads(
        back_pieces, pack_t, middle, routed, probability, chosen, grad_own, expert_gain[None, :],
        router_rows, ow_pieces,
    )
    mixed_grad = exchange_relative(mixed_grad, "shard")
    attention_grad, *mixed_grad = lax.optimization_barrier((attention_grad, *mixed_grad))
    far_grad, near_grad = swap(attention_grad, "shard", 2), swap(attention_grad, "shard", 1)
    mixed_grad_t = place_grads(mixed_grad, perm)

    w_heads = jnp.concatenate([w[h * head_size : (h + 1) * head_size] for h in range(heads) for w in w_rows], axis=0)
    bits = [1 << i for i in range(expert_devices.bit_length() - 1)]
    bits_first, bits_last = bits, [*bits[1:2], *bits[:1], *bits[2:]]
    high_first, high_last = bit_of(me_e, bits_first[0]).reshape(1), bit_of(me_e, bits_last[0]).reshape(1)
    head_grads, diagonals = [], []
    for h in range(heads):
        if h == heads - 1:
            keep_first, sent_first, gain_first, middle_grad_all = first_parts(
                normed, head_grads, w_rows, attention_grads, back, mixed_t, high_first
            )
            mixed_grad_t, sent_first, middle_grad_all = lax.optimization_barrier(
                (mixed_grad_t, sent_first, middle_grad_all)
            )
        head_grad, diagonal = attention_backward(qkv_t, bias_values, mixed_grad_t, h, heads, head_size)
        if h == 0:
            far_grad, near_grad, head_grad, result_own = together(far_grad, near_grad, head_grad, result_own)
            results = lax.all_gather(result_own, "shard", axis=0, tiled=True)
            attention_grads = [attention_grad, near_grad, far_grad, swap(far_grad, "shard", 1)]
        if h == heads - 1 and relative:
            sums_first = halving(keep_first, sent_first, "expert", bits_first)
            first, head_grad, diagonal = together(next(sums_first), head_grad, diagonal)
        head_grads.append(head_grad)
        diagonals.append(diagonal)
    qkv_grad_t = jnp.concatenate(head_grads, axis=0)

    normed_part = dot(qkv_grad_t, w_heads, 0, 0)
    half = length // 2
    low = me_s % 2
    other_half = lax.dynamic_slice_in_dim(normed_part, (1 - low) * half, half, 0)
    own_half = lax.dynamic_slice_in_dim(normed_part, low * half, half, 0)
    near_part = swap(other_half.astype(bf16), "shard", 1)
    if relative:
        first = sums_first.send(first)

    table_part = jnp.sum(jnp.where(bucket_flag[None], jnp.stack(diagonals), 0.0), axis=2).reshape(1, -1)
    table_part = jnp.pad(table_part, ((0, 0), (0, width - table_part.shape[1])))
    small = jnp.concatenate([jnp.zeros_like(table_part), expert_gain_part, router_part, table_part], axis=0)
    small = jnp.pad(small, ((0, -small.shape[0] % 64), (0, 0)))
    keep_last, sent_last = last_parts(
        normed, head_grads[-1], w_rows, heads - 1, gain_first, attention_gain[None, :], small, high_last
    )
    if relative:
        first, near_part, keep_last, results = together(first, near_part, keep_last, results)
        result = dot(back_absolute, results).astype(bf16)
        near_sum = (own_half + near_part.astype(f32)).astype(bf16)
        near_sum, sent_last = together(near_sum, sent_last)
        far_sum = swap(near_sum, "shard", 2)
        sums_last = halving(keep_last, sent_last, "expert", bits_last)
        first, last = together(sums_first.send(first), next(sums_last))
        for step in range(2 * len(bits) - 3):
            first, last = sums_first.send(first), sums_last.send(last)
            if step == 0:
                far_sum, first, last = together(far_sum, first, last)
            elif step == 1:
                result, first, last = together(result, first, last)
            else:
                first, last = together(first, last)
        first = sums_first.send(first)
        for _ in range(2):
            last = sums_last.send(last)
        last = sums_last.send(last)
    else:
        whole = []
        for keep, sent, high in ((keep_first, sent_first, high_first), (keep_last, sent_last, high_last)):
            sent = sent.astype(f32)
            low_part, high_part = jnp.where(high == 0, keep, sent), jnp.where(high == 0, sent, keep)
            low_part, high_part = lax.psum((low_part, high_part), "expert")
            whole.append((jnp.where(high == 0, low_part, high_part), jnp.where(high == 0, high_part, low_part)))
        first, last = whole
        near_sum = lax.optimization_barrier((own_half + near_part.astype(f32)).astype(bf16))
        far_sum = swap(near_sum, "shard", 2)
    if not relative:
        result = dot(back_absolute, results).astype(bf16)
    normed_grad = near_sum.astype(f32) + far_sum.astype(f32)
    source_half = lax.dynamic_slice_in_dim(inputs, low * half, half, 0).astype(f32)
    inverse_half = lax.rsqrt(jnp.mean(source_half * source_half, axis=-1, keepdims=True) + 1e-06)
    middle_half = lax.dynamic_slice_in_dim(middle_grad_all, low * half, half, 0).astype(f32)
    w = normed_grad * attention_gain
    grad_half = middle_half + inverse_half * w - source_half * (
        inverse_half * inverse_half * inverse_half * jnp.mean(w * source_half, axis=-1, keepdims=True)
    )
    grad_other = swap(grad_half, "shard", 1)
    input_gradient = place_halves(grad_half, grad_other, low)
    input_gradient, *last = together(input_gradient, *last)
    query_gradient, key_gradient, value_gradient, output_gradient = place_sums(
        first, last, jnp.concatenate([high_first, high_last]), heads, head_size
    )
    small = jnp.where(high_last == 0, last[1], last[0])[last[0].shape[0] - small.shape[0] :].astype(f32)
    table_gradient = small[2 + experts, : buckets * heads].reshape(heads, buckets).T
    small = sum_pairs(small[: 2 + experts], "shard")

    return (
        result,
        input_gradient,
        small[0],
        query_gradient.T,
        key_gradient.T,
        value_gradient.T,
        output_gradient,
        table_gradient,
        small[1],
        small[2:].T,
        in_gradient[None],
        out_gradient[None],
    )


def solution(mesh):
    placed = (
        P("expert", None),
        P("expert", None),
        P("expert"),
        P("expert"),
        P(),
        P(),
        P(None, "shard"),
        P(None, "shard"),
        P(None, "shard"),
        P("shard", None),
        P(None, "shard"),
        P(),
        P(),
        P("expert", None, "shard"),
        P("expert", "shard", None),
    )
    return jax.shard_map(
        on_device,
        mesh=mesh,
        in_specs=placed,
        out_specs=(
            P("expert", None),
            P("expert", None),
            P(),
            P(None, "shard"),
            P(None, "shard"),
            P(None, "shard"),
            P("shard", None),
            P(None, "shard"),
            P(),
            P(),
            P("expert", None, "shard"),
            P("expert", "shard", None),
        ),
        check_vma=False,
    )
```
